32 devices in a mesh: tm: 32 (over z, y, x, core).
Axes of the slice: x: 2, y: 2, z: 4, core: 2. Of those that a mesh axis runs over, the one named last changes fastest.
Arguments:
- transition: float32 [256, 128, 128], P('tm'), may hold values from -0.5 to 1
- obs_precision: float32 [256, 128], P('tm'), may hold values from 0.0001 to 0.001
- observations: float32 [256, 128], P('tm'), may hold values from -12 to 12
Outputs:
- smoothed: float32 [256, 128], P('tm')
The draws below stay inside these ranges and needn't reach their ends.
All inputs are finite; a program needn't handle non-finite values.
Results may differ from the reference program's by a relative error of at most 0.0004.
Values sent between devices are 32-bit elements; how exact they have to be, the bound alone decides.
No kernel may reach another device: no remote copies, remote signals or barrier semaphores. Data moves between devices by JAX's collectives and lax.ppermute only.
A program may use at most 64 MiB of HBM per device.

```python
import math
import jax
import jax.numpy as jnp
from jax import lax

LATENT_DIMENSION = 128
HORIZON_STEPS = 256


def draw_transition(key, part):
    key = jax.random.fold_in(key, 11)
    random_seed_pieces = jax.random.split(key, 5)
    base_exponent = jax.random.uniform(random_seed_pieces[0], (1, LATENT_DIMENSION), minval=-4.0, maxval=-3.0)
    jitter = jax.random.uniform(random_seed_pieces[1], (HORIZON_STEPS, LATENT_DIMENSION), minval=-0.3, maxval=0.3)
    transition_shrinkage = 1.0 - 10.0 ** (base_exponent + jitter)
    segment_matrix_entries = jax.random.randint(random_seed_pieces[2], (HORIZON_STEPS, 1), 0, max(HORIZON_STEPS // 4, 2)) == 0
    segment_edge = jax.random.uniform(random_seed_pieces[3], (HORIZON_STEPS, LATENT_DIMENSION), minval=0.5, maxval=0.8)
    transition_shrinkage = jnp.where(segment_matrix_entries, transition_shrinkage * segment_edge, transition_shrinkage)
    coupling_noise = jnp.clip(jax.random.normal(random_seed_pieces[4], (HORIZON_STEPS, LATENT_DIMENSION, LATENT_DIMENSION)), -6.0, 6.0)
    identity = jnp.eye(LATENT_DIMENSION, dtype=jnp.float32)
    scaled_noise = coupling_noise * (0.25 / LATENT_DIMENSION ** 0.5)
    return (scaled_noise * (1.0 - identity[None]) + transition_shrinkage[:, :, None] * identity[None]).astype(jnp.float32)


def levels(stream_key, dims, shards, low, largest):
    factor_of = 1.0
    for dim, shards_of in shards:
        heights = jax.random.uniform(jax.random.fold_in(jax.random.fold_in(stream_key, 6), dim), (shards_of,), jnp.float32, low / len(shards), largest / len(shards))
        factor_of = factor_of * jnp.repeat(jnp.exp(heights), dims[dim] // shards_of).reshape((-1,) + (1,) * (len(dims) - 1 - dim))
    return factor_of


def gaussian(stream_key, dims, width, most, cuts=(), held_as=jnp.bfloat16):
    loudness = levels(stream_key, dims, cuts, -0.22, 0.18) if cuts else 1.0
    array = jax.random.normal(stream_key, dims, jnp.float32) * width * loudness
    return jnp.minimum(jnp.maximum(array, -most), most).astype(held_as)


def setup_inputs(seed: int = 0) -> dict:
    key_list = jax.random.split(jax.random.key(seed), 4)
    transition = draw_transition(jax.random.fold_in(key_list[3], 71), 0)
    obs_precision = jnp.clip(jnp.exp(math.log(0.001) - 2.3025852 * jax.random.uniform(key_list[1], (HORIZON_STEPS, LATENT_DIMENSION), jnp.float32) ** levels(key_list[1], (HORIZON_STEPS, LATENT_DIMENSION), ((0, 32),), -0.2, 0.2)), 0.0001, 0.001)
    observations = gaussian(key_list[2], (HORIZON_STEPS, LATENT_DIMENSION), 2.0, 12.0, ((0, 32),), jnp.float32)
    return dict(transition=transition, obs_precision=obs_precision, observations=observations)


def reference(transition, obs_precision, observations):
    highest = lax.Precision.HIGHEST
    identity = jnp.eye(LATENT_DIMENSION, dtype=jnp.float32)
    information = obs_precision * observations

    def info_block(couple, inverse_covariance_band):
        return identity + inverse_covariance_band[:, None] * identity + jnp.dot(couple.T, couple, precision=highest)
    first_lower = jnp.linalg.cholesky(info_block(transition[0], obs_precision[0]))

    def forward(state_carry, inputs):
        lower_factor, vector = state_carry
        couple_here, inverse_covariance_band, target, couple_prev = inputs
        scaled_cols = jax.scipy.linalg.cho_solve((lower_factor, True), couple_prev.T)
        scaled_vec = jax.scipy.linalg.cho_solve((lower_factor, True), vector)
        pivot = info_block(couple_here, inverse_covariance_band) - jnp.dot(couple_prev, scaled_cols, precision=highest)
        carried = target + jnp.dot(couple_prev, scaled_vec, precision=highest)
        new_lower = jnp.linalg.cholesky(pivot)
        return ((new_lower, carried), (new_lower, carried))
    _, (lowers, vectors) = lax.scan(forward, (first_lower, information[0]), (transition[1:], obs_precision[1:], information[1:], transition[:-1]))
    lowers = jnp.concatenate([first_lower[None], lowers], axis=0)
    vectors = jnp.concatenate([information[0][None], vectors], axis=0)
    closing_value = jax.scipy.linalg.cho_solve((lowers[-1], True), vectors[-1])

    def backward(upper_value, inputs):
        lower_factor, vector, couple = inputs
        value = jax.scipy.linalg.cho_solve((lower_factor, True), vector + jnp.dot(couple.T, upper_value, precision=highest))
        return (value, value)
    _, values = lax.scan(backward, closing_value, (lowers[:-1], vectors[:-1], transition[:-1]), reverse=True)
    return jnp.concatenate([values, closing_value[None]], axis=0)
```

```python
import functools

import jax
import jax.numpy as jnp
from jax import lax
from jax.experimental import pallas as pl
from jax.experimental.pallas import tpu as pltpu
from jax.sharding import PartitionSpec as P

HIGHEST = lax.Precision.HIGHEST
PANEL = 16
ROWS = 8


def dot(left, right, contract=((1,), (0,))):
    return lax.dot_general(
        left, right, (contract, ((), ())), precision=HIGHEST, preferred_element_type=jnp.float32
    )


def inverses(matrices):
    n = matrices[0].shape[0]
    b = PANEL
    matrices = list(matrices)
    row_id = lax.broadcasted_iota(jnp.int32, (b, n), 0)
    lane_id = lax.broadcasted_iota(jnp.int32, (b, n), 1)
    full_lane = lax.broadcasted_iota(jnp.int32, (n, n), 1)
    for start in range(0, n, b):
        in_panel = (lane_id >= start) & (lane_id < start + b)
        eye = jnp.where(lane_id - start == row_id, 1.0, 0.0).astype(jnp.float32)
        rows = [m[start : start + b, :] for m in matrices]
        cols = [
            [jnp.broadcast_to(r[:, start + c : start + c + 1], (b, n)) for c in range(b)]
            for r in rows
        ]
        rows = [jnp.where(in_panel, eye, r) for r in rows]
        for j in range(b):
            pivot_row = row_id == j
            for q in range(len(matrices)):
                col = cols[q]
                inv = 1.0 / col[j][j : j + 1, :]
                coef = jnp.where(pivot_row, 1.0, -col[j])
                rows[q] = jnp.where(pivot_row, 0.0, rows[q]) + coef * (rows[q][j : j + 1, :] * inv)
                for c in range(j + 1, b):
                    col[c] = jnp.where(pivot_row, 0.0, col[c]) + coef * (col[c][j : j + 1, :] * inv)
        in_full = (full_lane >= start) & (full_lane < start + b)
        for q, m in enumerate(matrices):
            rest = jnp.where(in_full, 0.0, m) - dot(m[:, start : start + b], rows[q])
            parts = [rest[:start]] if start else []
            parts.append(rows[q])
            if start + b < n:
                parts.append(rest[start + b :])
            matrices[q] = jnp.concatenate(parts, axis=0)
    return matrices


def eliminated(inverse, sources):
    z = dot(sources, inverse)
    return z, dot(z, sources[: sources.shape[0] - ROWS], ((1,), (1,)))


def padded(row):
    return jnp.concatenate([row, jnp.zeros((ROWS - 1, row.shape[1]), jnp.float32)], axis=0)


def write_element(out_ref, n, alpha, gamma, beta, u, v):
    out_ref[0:n] = alpha
    out_ref[n : 2 * n] = gamma
    out_ref[2 * n : 3 * n] = beta
    out_ref[3 * n : 3 * n + ROWS] = jnp.concatenate(
        [u, v, jnp.zeros((ROWS - 2, n), jnp.float32)], axis=0
    )


def bit_of(axis, level):
    return lax.rem(lax.div(lax.axis_index(axis), 2**level), 2)


def local_kernel(trans_ref, prec_ref, obs_ref, elem_ref, z_ref):
    steps, n = prec_ref.shape
    row_id = lax.broadcasted_iota(jnp.int32, (n, n), 0)
    lane_id = lax.broadcasted_iota(jnp.int32, (n, n), 1)
    info = prec_ref[...] * obs_ref[...]
    centers = []
    for t in range(steps):
        a = trans_ref[t]
        scale = 1.0 + prec_ref[t : t + 1, :]
        centers.append(
            jnp.where(row_id == lane_id, scale, 0.0) + dot(a, a, ((0,), (0,)))
        )
    vectors = [info[t : t + 1, :] for t in range(steps)]
    forward = [trans_ref[t] for t in range(steps)]
    backward = [trans_ref[t].T if t % 2 == 0 else None for t in range(steps)]
    centers.append(jnp.zeros((n, n), jnp.float32))
    vectors.append(jnp.zeros((1, n), jnp.float32))
    slot = 0
    while len(forward) > 1:
        odd = range(1, len(forward), 2)
        invs = inverses([centers[j] for j in odd])
        new_forward, new_backward = [], []
        for inverse, j in zip(invs, odd):
            sources = jnp.concatenate([backward[j - 1], forward[j], padded(vectors[j])], axis=0)
            z, gram = eliminated(inverse, sources)
            z_ref[slot] = z
            slot += 1
            centers[j - 1] = centers[j - 1] - gram[0:n, 0:n]
            centers[j + 1] = centers[j + 1] - gram[n : 2 * n, n : 2 * n]
            vectors[j - 1] = vectors[j - 1] + gram[2 * n : 2 * n + 1, 0:n]
            vectors[j + 1] = vectors[j + 1] + gram[2 * n : 2 * n + 1, n : 2 * n]
            new_forward.append(gram[n : 2 * n, 0:n])
            new_backward.append(gram[0:n, n : 2 * n])
        forward, backward = new_forward, new_backward
        centers, vectors = centers[0::2], vectors[0::2]
    beta = jnp.where(bit_of("tm", 0) == 0, backward[0], forward[0])
    write_element(elem_ref, n, centers[0], centers[1], beta, vectors[0], vectors[1])


def merge_parts(level, mine_ref, theirs_ref):
    n = mine_ref.shape[1]
    is_left = bit_of("tm", level) == 0

    def part(lo, hi):
        m, t = mine_ref[lo:hi], theirs_ref[lo:hi]
        return jnp.where(is_left, m, t), jnp.where(is_left, t, m)

    alpha_l, alpha_r = part(0, n)
    gamma_l, gamma_r = part(n, 2 * n)
    beta_l, beta_r = part(2 * n, 3 * n)
    vec_l, vec_r = part(3 * n, 3 * n + ROWS)
    (inverse,) = inverses([alpha_r + gamma_l])
    target = vec_r[0:1] + vec_l[1:2]
    z, gram = eliminated(inverse, jnp.concatenate([beta_l, beta_r, padded(target)], axis=0))
    alpha = alpha_l - gram[0:n, 0:n]
    gamma = gamma_r - gram[n : 2 * n, n : 2 * n]
    u = vec_l[0:1] + gram[2 * n : 2 * n + 1, 0:n]
    v = vec_r[1:2] + gram[2 * n : 2 * n + 1, n : 2 * n]
    return z, alpha, gamma, gram[n : 2 * n, 0:n], gram[0:n, n : 2 * n], u, v


def merge_kernel(level, mine_ref, theirs_ref, elem_ref, z_ref):
    n = mine_ref.shape[1]
    z, alpha, gamma, beta, beta_t, u, v = merge_parts(level, mine_ref, theirs_ref)
    z_ref[...] = z
    chosen = jnp.where(bit_of("tm", level + 1) == 0, beta_t, beta)
    write_element(elem_ref, n, alpha, gamma, chosen, u, v)


def between(z_ref, index, low, high):
    n = low.shape[1]
    z = z_ref[index] if index is not None else z_ref[...]
    return (
        z[2 * n : 2 * n + 1]
        + dot(jnp.concatenate([low, high], axis=1), z[0 : 2 * n])
    )


def final_kernel(levels, steps, *refs):
    mine_ref, theirs_ref = refs[0:2]
    z_refs = refs[2 : 2 + levels - 1]
    local_ref = refs[2 + levels - 1]
    out_ref = refs[-1]
    n = mine_ref.shape[1]
    z, alpha, _, _, _, u, _ = merge_parts(levels - 1, mine_ref, theirs_ref)
    (first_inverse,) = inverses([alpha])
    low = dot(u, first_inverse)
    high = jnp.zeros((1, n), jnp.float32)
    middle = z[2 * n : 2 * n + 1] + dot(low, z[0:n])
    for level in range(levels - 1, -1, -1):
        if level < levels - 1:
            middle = between(z_refs[level], None, low, high)
        is_left = bit_of("tm", level) == 0
        low, high = jnp.where(is_left, low, middle), jnp.where(is_left, middle, high)
    states = {0: low, steps: high}
    slot = steps - 1
    gap = steps
    while gap > 1:
        slot -= steps // gap
        for k, start in enumerate(range(0, steps, gap)):
            states[start + gap // 2] = between(
                local_ref, slot + k, states[start], states[start + gap]
            )
        gap //= 2
    out_ref[...] = jnp.concatenate([states[t] for t in range(steps)], axis=0)


def body(transition, obs_precision, observations):
    steps, n = obs_precision.shape
    devices = lax.axis_size("tm")
    levels = devices.bit_length() - 1
    params = pltpu.CompilerParams(vmem_limit_bytes=48 * 2**20)
    element = jax.ShapeDtypeStruct((3 * n + ROWS, n), jnp.float32)
    z_shape = jax.ShapeDtypeStruct((2 * n + ROWS, n), jnp.float32)
    mine, local_z = pl.pallas_call(
        local_kernel,
        out_shape=(element, jax.ShapeDtypeStruct((steps - 1,) + z_shape.shape, jnp.float32)),
        compiler_params=params,
        name="local",
    )(transition, obs_precision, observations)
    zs = []
    for level in range(levels):
        theirs = lax.ppermute(mine, "tm", [(i, i ^ 2**level) for i in range(devices)])
        if level < levels - 1:
            mine, z = pl.pallas_call(
                functools.partial(merge_kernel, level),
                out_shape=(element, z_shape),
                compiler_params=params,
                name="merge",
            )(mine, theirs)
            zs.append(z)
    return pl.pallas_call(
        functools.partial(final_kernel, levels, steps),
        out_shape=jax.ShapeDtypeStruct((steps, n), jnp.float32),
        compiler_params=params,
        name="final",
    )(mine, theirs, *zs, local_z)


def solution(mesh):
    return jax.shard_map(
        body,
        mesh=mesh,
        in_specs=(P("tm", None, None), P("tm", None), P("tm", None)),
        out_specs=P("tm", None),
        check_vma=False,
    )
```

```python
import functools

import jax
import jax.numpy as jnp
from jax import lax
from jax.experimental import pallas as pl
from jax.experimental.pallas import tpu as pltpu
from jax.sharding import PartitionSpec as P

HIGHEST = lax.Precision.HIGHEST
PANEL = 16
ROWS = 8
SIDE_BY_SIDE = 4


def dot(left, right, contract=((1,), (0,))):
    return lax.dot_general(
        left, right, (contract, ((), ())), precision=HIGHEST, preferred_element_type=jnp.float32
    )


def spread(row):
    return jnp.broadcast_to(row, (ROWS, row.shape[1]))


def lane(tile, column):
    return jnp.broadcast_to(tile[:, column : column + 1], tile.shape)


def summed(terms):
    while len(terms) > 1:
        pairs = [terms[i] + terms[i + 1] for i in range(0, len(terms) - 1, 2)]
        terms = pairs + terms[len(pairs) * 2 :]
    return terms[0]


def panel_solved(cols, rows, masks):
    tiles = len(rows)
    scale = [None] * tiles
    for j in range(len(cols)):
        h, s = divmod(j, ROWS)
        inv = 1.0 / spread(cols[j][h][s : s + 1])
        scale[h] = inv if scale[h] is None else jnp.where(masks[s], inv, scale[h])
        factor = [cols[j][g] * inv for g in range(tiles)]
        factor[h] = jnp.where(masks[s], 0.0, factor[h])
        for c in range(j + 1, len(cols)):
            top = spread(cols[c][h][s : s + 1])
            for g in range(tiles):
                cols[c][g] = cols[c][g] - factor[g] * top
        top = spread(rows[h][s : s + 1])
        for g in range(tiles):
            rows[g] = rows[g] - factor[g] * top
    return [rows[g] * scale[g] for g in range(tiles)]


def inverses(matrices, ahead):
    n = matrices[0].shape[0]
    b = PANEL
    tiles = b // ROWS
    matrices = list(matrices)
    sub_id = lax.broadcasted_iota(jnp.int32, (ROWS, n), 0)
    lane_id = lax.broadcasted_iota(jnp.int32, (ROWS, n), 1)
    full_lane = lax.broadcasted_iota(jnp.int32, (n, n), 1)
    masks = [sub_id == j for j in range(ROWS)]

    def tiled(m, start):
        return [m[start + g * ROWS : start + (g + 1) * ROWS] for g in range(tiles)]

    panels = [tiled(m, 0) for m in matrices]
    for start in range(0, n, b):
        end = start + b
        in_panel = (lane_id >= start) & (lane_id < end)
        in_full = (full_lane >= start) & (full_lane < end)
        ready = []
        for panel in panels:
            cols = [[lane(panel[g], start + c) for g in range(tiles)] for c in range(b)]
            rows = [
                jnp.where(
                    in_panel, jnp.where(lane_id - start == sub_id + ROWS * g, 1.0, 0.0), panel[g]
                )
                for g in range(tiles)
            ]
            ready.append((cols, rows))
        solved = [panel_solved(cols, rows, masks) for cols, rows in ready]
        for q, m in enumerate(matrices):
            if ahead and end < n:
                panels[q] = [
                    jnp.where(in_panel, 0.0, t)
                    - summed(
                        [
                            lane(t, start + j) * spread(solved[q][j // ROWS][j % ROWS : j % ROWS + 1])
                            for j in range(b)
                        ]
                    )
                    for t in tiled(m, end)
                ]
            whole = jnp.concatenate(solved[q], axis=0)
            rest = jnp.where(in_full, 0.0, m) - dot(m[:, start:end], whole)
            parts = [rest[:start]] if start else []
            parts.append(whole)
            if end < n:
                if ahead:
                    parts += panels[q]
                    if end + b < n:
                        parts.append(rest[end + b :])
                else:
                    parts.append(rest[end:])
                    panels[q] = tiled(rest, end)
            matrices[q] = jnp.concatenate(parts, axis=0)
    return matrices


def eliminated(inverse, sources):
    z = dot(sources, inverse)
    return z, dot(z, sources[: sources.shape[0] - ROWS], ((1,), (1,)))


def padded(row):
    return jnp.concatenate([row, jnp.zeros((ROWS - 1, row.shape[1]), jnp.float32)], axis=0)


def write_element(out_ref, n, alpha, gamma, beta, u, v):
    out_ref[0:n] = alpha
    out_ref[n : 2 * n] = gamma
    out_ref[2 * n : 3 * n] = beta
    out_ref[3 * n : 3 * n + ROWS] = jnp.concatenate(
        [u, v, jnp.zeros((ROWS - 2, n), jnp.float32)], axis=0
    )


def bit_of(axis, level):
    return lax.rem(lax.div(lax.axis_index(axis), 2**level), 2)


def local_kernel(
    trans_hbm, prec_hbm, obs_hbm, elem_ref, z_ref,
    prec_ref, obs_ref, center_ref, inv_ref, fwd_ref, bwd_ref, vec_ref, sems,
):
    steps, n = prec_ref.shape
    always = lax.axis_index("tm") >= 0
    small = [
        pltpu.make_async_copy(prec_hbm, prec_ref, sems.at[steps]),
        pltpu.make_async_copy(obs_hbm, obs_ref, sems.at[steps + 1]),
    ]
    large = [
        pltpu.make_async_copy(trans_hbm.at[t], fwd_ref.at[t], sems.at[t]) for t in range(steps)
    ]
    for copy in small + large:
        copy.start()
    for copy in small:
        copy.wait()

    @pl.when(always)
    def _():
        row_id = lax.broadcasted_iota(jnp.int32, (n, n), 0)
        lane_id = lax.broadcasted_iota(jnp.int32, (n, n), 1)
        for t in range(steps):
            large[t].wait()
            a = fwd_ref[t]
            scale = 1.0 + prec_ref[t : t + 1, :]
            center_ref[t] = jnp.where(row_id == lane_id, scale, 0.0) + dot(a, a, ((0,), (0,)))
            if t % 2 == 0:
                bwd_ref[t] = a.T
        center_ref[steps] = jnp.zeros((n, n), jnp.float32)
        vec_ref[0:steps] = prec_ref[...] * obs_ref[...]
        vec_ref[steps : steps + 1] = jnp.zeros((1, n), jnp.float32)

    slot = 0
    gap = 1
    while gap < steps:
        odd = list(range(gap, steps, 2 * gap))
        for first in range(0, len(odd), SIDE_BY_SIDE):
            group = odd[first : first + SIDE_BY_SIDE]

            @pl.when(always)
            def _(group=group):
                for j, inverse in zip(group, inverses([center_ref[j] for j in group], len(group) <= 2)):
                    inv_ref[j] = inverse

        @pl.when(always)
        def _(odd=odd, gap=gap, slot=slot):
            for k, j in enumerate(odd):
                low, high = j - gap, j + gap
                sources = jnp.concatenate(
                    [bwd_ref[low], fwd_ref[j], padded(vec_ref[j : j + 1])], axis=0
                )
                z, gram = eliminated(inv_ref[j], sources)
                z_ref[slot + k] = z
                center_ref[low] = center_ref[low] - gram[0:n, 0:n]
                center_ref[high] = center_ref[high] - gram[n : 2 * n, n : 2 * n]
                vec_ref[low : low + 1] = vec_ref[low : low + 1] + gram[2 * n : 2 * n + 1, 0:n]
                vec_ref[high : high + 1] = (
                    vec_ref[high : high + 1] + gram[2 * n : 2 * n + 1, n : 2 * n]
                )
                fwd_ref[low] = gram[n : 2 * n, 0:n]
                bwd_ref[low] = gram[0:n, n : 2 * n]

        slot += len(odd)
        gap *= 2
    beta = jnp.where(bit_of("tm", 0) == 0, bwd_ref[0], fwd_ref[0])
    write_element(
        elem_ref, n, center_ref[0], center_ref[steps], beta, vec_ref[0:1], vec_ref[steps : steps + 1]
    )


def merge_parts(level, mine_ref, theirs_ref):
    n = mine_ref.shape[1]
    is_left = bit_of("tm", level) == 0

    def part(lo, hi):
        m, t = mine_ref[lo:hi], theirs_ref[lo:hi]
        return jnp.where(is_left, m, t), jnp.where(is_left, t, m)

    alpha_l, alpha_r = part(0, n)
    gamma_l, gamma_r = part(n, 2 * n)
    beta_l, beta_r = part(2 * n, 3 * n)
    vec_l, vec_r = part(3 * n, 3 * n + ROWS)
    (inverse,) = inverses([alpha_r + gamma_l], True)
    target = vec_r[0:1] + vec_l[1:2]
    z, gram = eliminated(inverse, jnp.concatenate([beta_l, beta_r, padded(target)], axis=0))
    alpha = alpha_l - gram[0:n, 0:n]
    gamma = gamma_r - gram[n : 2 * n, n : 2 * n]
    u = vec_l[0:1] + gram[2 * n : 2 * n + 1, 0:n]
    v = vec_r[1:2] + gram[2 * n : 2 * n + 1, n : 2 * n]
    return z, alpha, gamma, gram[n : 2 * n, 0:n], gram[0:n, n : 2 * n], u, v


def merge_kernel(level, mine_ref, theirs_ref, elem_ref, z_ref):
    n = mine_ref.shape[1]
    z, alpha, gamma, beta, beta_t, u, v = merge_parts(level, mine_ref, theirs_ref)
    z_ref[...] = z
    chosen = jnp.where(bit_of("tm", level + 1) == 0, beta_t, beta)
    write_element(elem_ref, n, alpha, gamma, chosen, u, v)


def closing_kernel(level, mine_ref, theirs_ref, small_ref, z_ref, first_ref):
    n = mine_ref.shape[1]
    z, alpha, gamma, beta, _, u, v = merge_parts(level, mine_ref, theirs_ref)
    z_ref[...] = z
    (inverse,) = inverses([alpha], True)
    first = dot(jnp.concatenate([beta, padded(u)], axis=0), inverse)
    first_ref[...] = first
    gram = dot(first, beta, ((1,), (1,)))
    is_lower = bit_of("tm", level + 1) == 0
    small_ref[0:n] = jnp.where(is_lower, gamma - gram[0:n], alpha)
    small_ref[n : n + ROWS] = padded(jnp.where(is_lower, v + gram[n : n + 1], u))


def between(z, low, high):
    n = low.shape[1]
    return z[2 * n : 2 * n + 1] + dot(jnp.concatenate([low, high], axis=1), z[0 : 2 * n])


def final_kernel(levels, steps, *refs):
    mine_ref, theirs_ref = refs[0:2]
    z_refs = refs[2 : levels + 1]
    first_ref, local_ref, out_ref = refs[levels + 1 :]
    n = mine_ref.shape[1]
    (inverse,) = inverses([mine_ref[0:n] + theirs_ref[0:n]], True)
    middle = dot(mine_ref[n : n + 1] + theirs_ref[n : n + 1], inverse)
    first = first_ref[n : n + 1] + dot(middle, first_ref[0:n])
    is_lower = bit_of("tm", levels - 1) == 0
    low = jnp.where(is_lower, first, middle)
    high = jnp.where(is_lower, middle, 0.0)
    for level in range(levels - 2, -1, -1):
        middle = between(z_refs[level], low, high)
        is_left = bit_of("tm", level) == 0
        low, high = jnp.where(is_left, low, middle), jnp.where(is_left, middle, high)
    states = {0: low, steps: high}
    slot = steps - 1
    gap = steps
    while gap > 1:
        slot -= steps // gap
        for k, start in enumerate(range(0, steps, gap)):
            states[start + gap // 2] = between(
                local_ref.at[slot + k], states[start], states[start + gap]
            )
        gap //= 2
    out_ref[...] = jnp.concatenate([states[t] for t in range(steps)], axis=0)


def body(transition, obs_precision, observations):
    steps, n = obs_precision.shape
    devices = lax.axis_size("tm")
    levels = devices.bit_length() - 1
    params = pltpu.CompilerParams(vmem_limit_bytes=48 * 2**20)
    element = jax.ShapeDtypeStruct((3 * n + ROWS, n), jnp.float32)
    z_shape = jax.ShapeDtypeStruct((2 * n + ROWS, n), jnp.float32)
    mine, local_z = pl.pallas_call(
        local_kernel,
        out_shape=(element, jax.ShapeDtypeStruct((steps - 1,) + z_shape.shape, jnp.float32)),
        in_specs=[pl.BlockSpec(memory_space=pl.ANY)] * 3,
        scratch_shapes=[
            pltpu.VMEM((steps, n), jnp.float32),
            pltpu.VMEM((steps, n), jnp.float32),
            pltpu.VMEM((steps + 1, n, n), jnp.float32),
            pltpu.VMEM((steps, n, n), jnp.float32),
            pltpu.VMEM((steps, n, n), jnp.float32),
            pltpu.VMEM((steps, n, n), jnp.float32),
            pltpu.VMEM((2 * steps, n), jnp.float32),
            pltpu.SemaphoreType.DMA((steps + 2,)),
        ],
        compiler_params=params,
        name="local",
    )(transition, obs_precision, observations)
    zs = []
    small = jax.ShapeDtypeStruct((n + ROWS, n), jnp.float32)

    def exchanged(array, level):
        return lax.ppermute(array, "tm", [(i, i ^ 2**level) for i in range(devices)])

    for level in range(levels - 2):
        mine, z = pl.pallas_call(
            functools.partial(merge_kernel, level),
            out_shape=(element, z_shape),
            compiler_params=params,
            name="merge",
        )(mine, exchanged(mine, level))
        zs.append(z)
    last, z, first = pl.pallas_call(
        functools.partial(closing_kernel, levels - 2),
        out_shape=(small, z_shape, small),
        compiler_params=params,
        name="closing",
    )(mine, exchanged(mine, levels - 2))
    return pl.pallas_call(
        functools.partial(final_kernel, levels, steps),
        out_shape=jax.ShapeDtypeStruct((steps, n), jnp.float32),
        compiler_params=params,
        name="final",
    )(last, exchanged(last, levels - 1), *zs, z, first, local_z)


def solution(mesh):
    return jax.shard_map(
        body,
        mesh=mesh,
        in_specs=(P("tm", None, None), P("tm", None), P("tm", None)),
        out_specs=P("tm", None),
        check_vma=False,
    )
```

```python
import functools

import jax
import jax.numpy as jnp
from jax import lax
from jax.experimental import pallas as pl
from jax.experimental.pallas import tpu as pltpu
from jax.sharding import PartitionSpec as P

HIGHEST = lax.Precision.HIGHEST
PANEL = 16
ROWS = 8
SIDE_BY_SIDE = 4


def dot(left, right, contract=((1,), (0,))):
    return lax.dot_general(
        left, right, (contract, ((), ())), precision=HIGHEST, preferred_element_type=jnp.float32
    )


def spread(row):
    return jnp.broadcast_to(row, (ROWS, row.shape[1]))


def lane(tile, column):
    return jnp.broadcast_to(tile[:, column : column + 1], tile.shape)


def summed(terms):
    while len(terms) > 1:
        pairs = [terms[i] + terms[i + 1] for i in range(0, len(terms) - 1, 2)]
        terms = pairs + terms[len(pairs) * 2 :]
    return terms[0]


def panel_solved(cols, rows, masks):
    tiles = len(rows)
    scale = [None] * tiles
    for j in range(len(cols)):
        h, s = divmod(j, ROWS)
        inv = 1.0 / spread(cols[j][h][s : s + 1])
        scale[h] = inv if scale[h] is None else jnp.where(masks[s], inv, scale[h])
        factor = [cols[j][g] * inv for g in range(tiles)]
        factor[h] = jnp.where(masks[s], 0.0, factor[h])
        for c in range(j + 1, len(cols)):
            top = spread(cols[c][h][s : s + 1])
            for g in range(tiles):
                cols[c][g] = cols[c][g] - factor[g] * top
        top = spread(rows[h][s : s + 1])
        for g in range(tiles):
            rows[g] = rows[g] - factor[g] * top
    return [rows[g] * scale[g] for g in range(tiles)]


def inverses(matrices, ahead):
    n = matrices[0].shape[0]
    b = PANEL
    tiles = b // ROWS
    matrices = list(matrices)
    sub_id = lax.broadcasted_iota(jnp.int32, (ROWS, n), 0)
    lane_id = lax.broadcasted_iota(jnp.int32, (ROWS, n), 1)
    full_lane = lax.broadcasted_iota(jnp.int32, (n, n), 1)
    masks = [sub_id == j for j in range(ROWS)]

    def tiled(m, start):
        return [m[start + g * ROWS : start + (g + 1) * ROWS] for g in range(tiles)]

    panels = [tiled(m, 0) for m in matrices]
    for start in range(0, n, b):
        end = start + b
        in_panel = (lane_id >= start) & (lane_id < end)
        in_full = (full_lane >= start) & (full_lane < end)
        ready = []
        for panel in panels:
            cols = [[lane(panel[g], start + c) for g in range(tiles)] for c in range(b)]
            rows = [
                jnp.where(
                    in_panel, jnp.where(lane_id - start == sub_id + ROWS * g, 1.0, 0.0), panel[g]
                )
                for g in range(tiles)
            ]
            ready.append((cols, rows))
        solved = [panel_solved(cols, rows, masks) for cols, rows in ready]
        for q, m in enumerate(matrices):
            if ahead and end < n:
                panels[q] = [
                    jnp.where(in_panel, 0.0, t)
                    - summed(
                        [
                            lane(t, start + j) * spread(solved[q][j // ROWS][j % ROWS : j % ROWS + 1])
                            for j in range(b)
                        ]
                    )
                    for t in tiled(m, end)
                ]
            whole = jnp.concatenate(solved[q], axis=0)
            rest = jnp.where(in_full, 0.0, m) - dot(m[:, start:end], whole)
            parts = [rest[:start]] if start else []
            parts.append(whole)
            if end < n:
                if ahead:
                    parts += panels[q]
                    if end + b < n:
                        parts.append(rest[end + b :])
                else:
                    parts.append(rest[end:])
                    panels[q] = tiled(rest, end)
            matrices[q] = jnp.concatenate(parts, axis=0)
    return matrices


def eliminated(inverse, sources):
    z = dot(sources, inverse)
    return z, dot(z, sources[: sources.shape[0] - ROWS], ((1,), (1,)))


def padded(row):
    return jnp.concatenate([row, jnp.zeros((ROWS - 1, row.shape[1]), jnp.float32)], axis=0)


def write_near(is_left, near_ref, alpha, gamma, u, v):
    n = alpha.shape[0]
    near_ref[0:n] = jnp.where(is_left, gamma, alpha)
    near_ref[n : n + ROWS] = padded(jnp.where(is_left, v, u))


def write_far(is_left, far_ref, alpha, gamma, beta_t, beta, u, v):
    n = alpha.shape[0]
    far_ref[0:n] = jnp.where(is_left, alpha, gamma)
    far_ref[n : 2 * n] = jnp.where(is_left, beta_t, beta)
    far_ref[2 * n : 2 * n + ROWS] = padded(jnp.where(is_left, u, v))


def bit_of(axis, level):
    return lax.rem(lax.div(lax.axis_index(axis), 2**level), 2)


def local_kernel(
    trans_hbm, prec_hbm, obs_hbm, near_ref, far_ref, z_ref,
    prec_ref, obs_ref, center_ref, inv_ref, fwd_ref, bwd_ref, vec_ref, sems,
):
    steps, n = prec_ref.shape
    always = lax.axis_index("tm") >= 0
    copies = [
        pltpu.make_async_copy(trans_hbm, fwd_ref, sems.at[0]),
        pltpu.make_async_copy(prec_hbm, prec_ref, sems.at[1]),
        pltpu.make_async_copy(obs_hbm, obs_ref, sems.at[2]),
    ]
    for copy in copies:
        copy.start()
    for copy in copies:
        copy.wait()

    @pl.when(always)
    def _():
        row_id = lax.broadcasted_iota(jnp.int32, (n, n), 0)
        lane_id = lax.broadcasted_iota(jnp.int32, (n, n), 1)
        for t in range(steps):
            a = fwd_ref[t]
            scale = 1.0 + prec_ref[t : t + 1, :]
            center_ref[t] = jnp.where(row_id == lane_id, scale, 0.0) + dot(a, a, ((0,), (0,)))
            if t % 2 == 0:
                bwd_ref[t] = a.T
        center_ref[steps] = jnp.zeros((n, n), jnp.float32)
        vec_ref[0:steps] = prec_ref[...] * obs_ref[...]
        vec_ref[steps : steps + 1] = jnp.zeros((1, n), jnp.float32)

    slot = 0
    gap = 1
    while gap < steps:
        odd = list(range(gap, steps, 2 * gap))
        for first in range(0, len(odd), SIDE_BY_SIDE):
            group = odd[first : first + SIDE_BY_SIDE]

            @pl.when(always)
            def _(group=group):
                for j, inverse in zip(group, inverses([center_ref[j] for j in group], len(group) <= 2)):
                    inv_ref[j] = inverse

        @pl.when(always)
        def _(odd=odd, gap=gap, slot=slot):
            for k, j in enumerate(odd):
                low, high = j - gap, j + gap
                sources = jnp.concatenate(
                    [bwd_ref[low], fwd_ref[j], padded(vec_ref[j : j + 1])], axis=0
                )
                z, gram = eliminated(inv_ref[j], sources)
                z_ref[slot + k] = z
                center_ref[low] = center_ref[low] - gram[0:n, 0:n]
                center_ref[high] = center_ref[high] - gram[n : 2 * n, n : 2 * n]
                vec_ref[low : low + 1] = vec_ref[low : low + 1] + gram[2 * n : 2 * n + 1, 0:n]
                vec_ref[high : high + 1] = (
                    vec_ref[high : high + 1] + gram[2 * n : 2 * n + 1, n : 2 * n]
                )
                fwd_ref[low] = gram[n : 2 * n, 0:n]
                bwd_ref[low] = gram[0:n, n : 2 * n]

        slot += len(odd)
        gap *= 2
    is_left = bit_of("tm", 0) == 0
    alpha, gamma, u, v = center_ref[0], center_ref[steps], vec_ref[0:1], vec_ref[steps : steps + 1]
    write_near(is_left, near_ref, alpha, gamma, u, v)
    write_far(is_left, far_ref, alpha, gamma, bwd_ref[0], fwd_ref[0], u, v)


def inverse_kernel(near_ref, came_near_ref, inv_ref):
    n = near_ref.shape[1]
    inv_ref[...] = inverses([near_ref[0:n] + came_near_ref[0:n]], True)[0]


def parts(level, far_ref, came_far_ref):
    n = far_ref.shape[1]
    is_left = bit_of("tm", level) == 0

    def part(lo, hi):
        m, t = far_ref[lo:hi], came_far_ref[lo:hi]
        return jnp.where(is_left, m, t), jnp.where(is_left, t, m)

    return (*part(0, n), *part(n, 2 * n), *part(2 * n, 2 * n + ROWS))


def near_kernel(level, inv_ref, near_ref, came_near_ref, far_ref, came_far_ref, near_out):
    n = near_ref.shape[1]
    alpha, gamma, beta_low, beta_high, u, v = parts(level, far_ref, came_far_ref)
    next_left = bit_of("tm", level + 1) == 0
    beta = jnp.where(next_left, beta_high, beta_low)
    target = near_ref[n : n + ROWS] + came_near_ref[n : n + ROWS]
    gram = dot(
        dot(jnp.concatenate([beta, target], axis=0), inv_ref[...]), beta, ((1,), (1,))
    )
    near_out[0:n] = jnp.where(next_left, gamma, alpha) - gram[0:n]
    near_out[n : n + ROWS] = jnp.where(next_left, v, u) + gram[n : n + ROWS]


def merged(level, inv_ref, near_ref, came_near_ref, far_ref, came_far_ref):
    n = near_ref.shape[1]
    alpha, gamma, beta_low, beta_high, u, v = parts(level, far_ref, came_far_ref)
    target = near_ref[n : n + ROWS] + came_near_ref[n : n + ROWS]
    z, gram = eliminated(inv_ref[...], jnp.concatenate([beta_low, beta_high, target], axis=0))
    return (
        z,
        alpha - gram[0:n, 0:n],
        gamma - gram[n : 2 * n, n : 2 * n],
        gram[0:n, n : 2 * n],
        gram[n : 2 * n, 0:n],
        u[0:1] + gram[2 * n : 2 * n + 1, 0:n],
        v[0:1] + gram[2 * n : 2 * n + 1, n : 2 * n],
    )


def far_kernel(level, *refs):
    far_out, z_ref = refs[6:]
    z, alpha, gamma, beta_t, beta, u, v = merged(level, *refs[:5])
    z_ref[...] = z
    write_far(bit_of("tm", level + 1) == 0, far_out, alpha, gamma, beta_t, beta, u, v)


def closing_kernel(level, *refs):
    small_ref, z_ref, first_ref = refs[5:]
    z, alpha, gamma, _, beta, u, v = merged(level, *refs[:5])
    n = alpha.shape[0]
    z_ref[...] = z
    (inverse,) = inverses([alpha], True)
    first = dot(jnp.concatenate([beta, padded(u)], axis=0), inverse)
    first_ref[...] = first
    gram = dot(first, beta, ((1,), (1,)))
    is_lower = bit_of("tm", level + 1) == 0
    small_ref[0:n] = jnp.where(is_lower, gamma - gram[0:n], alpha)
    small_ref[n : n + ROWS] = padded(jnp.where(is_lower, v + gram[n : n + 1], u))


def between(z, low, high):
    n = low.shape[1]
    return z[2 * n : 2 * n + 1] + dot(jnp.concatenate([low, high], axis=1), z[0 : 2 * n])


def final_kernel(levels, steps, *refs):
    mine_ref, theirs_ref = refs[0:2]
    z_refs = refs[2 : levels + 1]
    first_ref, local_ref, out_ref = refs[levels + 1 :]
    n = mine_ref.shape[1]
    (inverse,) = inverses([mine_ref[0:n] + theirs_ref[0:n]], True)
    middle = dot(mine_ref[n : n + 1] + theirs_ref[n : n + 1], inverse)
    first = first_ref[n : n + 1] + dot(middle, first_ref[0:n])
    is_lower = bit_of("tm", levels - 1) == 0
    low = jnp.where(is_lower, first, middle)
    high = jnp.where(is_lower, middle, 0.0)
    for level in range(levels - 2, -1, -1):
        middle = between(z_refs[level], low, high)
        is_left = bit_of("tm", level) == 0
        low, high = jnp.where(is_left, low, middle), jnp.where(is_left, middle, high)
    states = {0: low, steps: high}
    slot = steps - 1
    gap = steps
    while gap > 1:
        slot -= steps // gap
        for k, start in enumerate(range(0, steps, gap)):
            states[start + gap // 2] = between(
                local_ref.at[slot + k], states[start], states[start + gap]
            )
        gap //= 2
    out_ref[...] = jnp.concatenate([states[t] for t in range(steps)], axis=0)


def body(transition, obs_precision, observations):
    steps, n = obs_precision.shape
    devices = lax.axis_size("tm")
    levels = devices.bit_length() - 1
    params = pltpu.CompilerParams(vmem_limit_bytes=48 * 2**20)
    small = jax.ShapeDtypeStruct((n + ROWS, n), jnp.float32)
    large = jax.ShapeDtypeStruct((2 * n + ROWS, n), jnp.float32)
    square = jax.ShapeDtypeStruct((n, n), jnp.float32)
    near, far, local_z = pl.pallas_call(
        local_kernel,
        out_shape=(small, large, jax.ShapeDtypeStruct((steps - 1,) + large.shape, jnp.float32)),
        in_specs=[pl.BlockSpec(memory_space=pltpu.HBM)] * 3,
        scratch_shapes=[
            pltpu.VMEM((steps, n), jnp.float32),
            pltpu.VMEM((steps, n), jnp.float32),
            pltpu.VMEM((steps + 1, n, n), jnp.float32),
            pltpu.VMEM((steps, n, n), jnp.float32),
            pltpu.VMEM((steps, n, n), jnp.float32),
            pltpu.VMEM((steps, n, n), jnp.float32),
            pltpu.VMEM((2 * steps, n), jnp.float32),
            pltpu.SemaphoreType.DMA((3,)),
        ],
        compiler_params=pltpu.CompilerParams(vmem_limit_bytes=60 * 2**20),
        name="local",
    )(transition, obs_precision, observations)
    zs = []

    def exchanged(array, level):
        return lax.ppermute(array, "tm", [(i, i ^ 2**level) for i in range(devices)])

    def called(kernel, out_shape, name, flops, *arrays):
        whole = pl.BlockSpec(memory_space=pltpu.VMEM)
        unread = pl.BlockSpec(memory_space=pl.ANY)
        return pl.pallas_call(
            kernel,
            out_shape=out_shape,
            in_specs=[whole] * 5 + [unread] if len(arrays) == 6 else [whole] * len(arrays),
            compiler_params=params,
            cost_estimate=pl.CostEstimate(
                flops=flops, bytes_accessed=12 * n * n, transcendentals=0
            ),
            name=name,
        )(*arrays)

    for level in range(levels - 1):
        came_near = exchanged(near, level)
        came_far = exchanged(far, level)
        inverse = called(inverse_kernel, square, "inverse", 3000 * n**3, near, came_near)
        held = (inverse, near, came_near, far, came_far)
        if level < levels - 2:
            near = called(
                functools.partial(near_kernel, level), small, "near", 500 * n**3, *held
            )
            far, z = called(
                functools.partial(far_kernel, level), (large, large), "far", 700 * n**3, *held, near
            )
        else:
            near, z, first = called(
                functools.partial(closing_kernel, level), (small, large, small), "closing", 2000 * n**3, *held
            )
        zs.append(z)
    return pl.pallas_call(
        functools.partial(final_kernel, levels, steps),
        out_shape=jax.ShapeDtypeStruct((steps, n), jnp.float32),
        compiler_params=params,
        name="final",
    )(near, exchanged(near, levels - 1), *zs, first, local_z)


def solution(mesh):
    return jax.shard_map(
        body,
        mesh=mesh,
        in_specs=(P("tm", None, None), P("tm", None), P("tm", None)),
        out_specs=P("tm", None),
        check_vma=False,
    )
```

```python
import functools

import jax
import jax.numpy as jnp
from jax import lax
from jax.experimental import pallas as pl
from jax.experimental.pallas import tpu as pltpu
from jax.sharding import PartitionSpec as P

HIGHEST = lax.Precision.HIGHEST
PANEL = 16
ROWS = 8
SIDE_BY_SIDE = 4


def dot(left, right, contract=((1,), (0,))):
    return lax.dot_general(
        left, right, (contract, ((), ())), precision=HIGHEST, preferred_element_type=jnp.float32
    )


def spread(row):
    return jnp.broadcast_to(row, (ROWS, row.shape[1]))


def lane(tile, column):
    return jnp.broadcast_to(tile[:, column : column + 1], tile.shape)


def summed(terms):
    while len(terms) > 1:
        pairs = [terms[i] + terms[i + 1] for i in range(0, len(terms) - 1, 2)]
        terms = pairs + terms[len(pairs) * 2 :]
    return terms[0]


def panel_solved(cols, rows, masks):
    tiles = len(rows)
    scale = [None] * tiles
    for j in range(len(cols)):
        h, s = divmod(j, ROWS)
        inv = 1.0 / spread(cols[j][h][s : s + 1])
        scale[h] = inv if scale[h] is None else jnp.where(masks[s], inv, scale[h])
        factor = [cols[j][g] * inv for g in range(tiles)]
        factor[h] = jnp.where(masks[s], 0.0, factor[h])
        for c in range(j + 1, len(cols)):
            top = spread(cols[c][h][s : s + 1])
            for g in range(tiles):
                cols[c][g] = cols[c][g] - factor[g] * top
        top = spread(rows[h][s : s + 1])
        for g in range(tiles):
            rows[g] = rows[g] - factor[g] * top
    return [rows[g] * scale[g] for g in range(tiles)]


def inverses(matrices, ahead):
    n = matrices[0].shape[0]
    b = PANEL
    tiles = b // ROWS
    matrices = list(matrices)
    sub_id = lax.broadcasted_iota(jnp.int32, (ROWS, n), 0)
    lane_id = lax.broadcasted_iota(jnp.int32, (ROWS, n), 1)
    full_lane = lax.broadcasted_iota(jnp.int32, (n, n), 1)
    masks = [sub_id == j for j in range(ROWS)]

    def tiled(m, start):
        return [m[start + g * ROWS : start + (g + 1) * ROWS] for g in range(tiles)]

    panels = [tiled(m, 0) for m in matrices]
    for start in range(0, n, b):
        end = start + b
        in_panel = (lane_id >= start) & (lane_id < end)
        in_full = (full_lane >= start) & (full_lane < end)
        ready = []
        for panel in panels:
            cols = [[lane(panel[g], start + c) for g in range(tiles)] for c in range(b)]
            rows = [
                jnp.where(
                    in_panel, jnp.where(lane_id - start == sub_id + ROWS * g, 1.0, 0.0), panel[g]
                )
                for g in range(tiles)
            ]
            ready.append((cols, rows))
        solved = [panel_solved(cols, rows, masks) for cols, rows in ready]
        for q, m in enumerate(matrices):
            if ahead and end < n:
                panels[q] = [
                    jnp.where(in_panel, 0.0, t)
                    - summed(
                        [
                            lane(t, start + j) * spread(solved[q][j // ROWS][j % ROWS : j % ROWS + 1])
                            for j in range(b)
                        ]
                    )
                    for t in tiled(m, end)
                ]
            whole = jnp.concatenate(solved[q], axis=0)
            rest = jnp.where(in_full, 0.0, m) - dot(m[:, start:end], whole)
            parts = [rest[:start]] if start else []
            parts.append(whole)
            if end < n:
                if ahead:
                    parts += panels[q]
                    if end + b < n:
                        parts.append(rest[end + b :])
                else:
                    parts.append(rest[end:])
                    panels[q] = tiled(rest, end)
            matrices[q] = jnp.concatenate(parts, axis=0)
    return matrices


def eliminated(inverse, sources):
    z = dot(sources, inverse)
    return z, dot(z, sources[: sources.shape[0] - ROWS], ((1,), (1,)))


def padded(row):
    return jnp.concatenate([row, jnp.zeros((ROWS - 1, row.shape[1]), jnp.float32)], axis=0)


def write_near(is_left, near_ref, alpha, gamma, u, v):
    n = alpha.shape[0]
    near_ref[0:n] = jnp.where(is_left, gamma, alpha)
    near_ref[n : n + ROWS] = padded(jnp.where(is_left, v, u))


def write_far(is_left, far_ref, alpha, gamma, beta_t, beta, u, v):
    n = alpha.shape[0]
    far_ref[0:n] = jnp.where(is_left, alpha, gamma)
    far_ref[n : 2 * n] = jnp.where(is_left, beta_t, beta)
    far_ref[2 * n : 2 * n + ROWS] = padded(jnp.where(is_left, u, v))


def bit_of(axis, level):
    return lax.rem(lax.div(lax.axis_index(axis), 2**level), 2)


def local_kernel(
    trans_hbm, prec_hbm, obs_hbm, near_ref, far_ref, z_hbm,
    z_ref, prec_ref, obs_ref, center_ref, inv_ref, fwd_ref, bwd_ref, vec_ref, sems,
):
    steps, n = prec_ref.shape
    always = lax.axis_index("tm") >= 0
    copies = [
        pltpu.make_async_copy(trans_hbm, fwd_ref, sems.at[0]),
        pltpu.make_async_copy(prec_hbm, prec_ref, sems.at[1]),
        pltpu.make_async_copy(obs_hbm, obs_ref, sems.at[2]),
    ]
    for copy in copies:
        copy.start()
    for copy in copies:
        copy.wait()

    def center(t):
        row_id = lax.broadcasted_iota(jnp.int32, (n, n), 0)
        lane_id = lax.broadcasted_iota(jnp.int32, (n, n), 1)
        a = fwd_ref[t]
        scale = 1.0 + prec_ref[t : t + 1, :]
        return jnp.where(row_id == lane_id, scale, 0.0) + dot(a, a, ((0,), (0,)))

    @pl.when(always)
    def _():
        for t in range(1, steps, 2):
            center_ref[t] = center(t)
        center_ref[steps] = jnp.zeros((n, n), jnp.float32)
        vec_ref[0:steps] = prec_ref[...] * obs_ref[...]
        vec_ref[steps : steps + 1] = jnp.zeros((1, n), jnp.float32)

    slot = 0
    gap = 1
    leaving = []
    while gap < steps:
        odd = list(range(gap, steps, 2 * gap))
        for first in range(0, len(odd), SIDE_BY_SIDE):
            group = odd[first : first + SIDE_BY_SIDE]

            @pl.when(always)
            def _(group=group, gap=gap):
                if gap == 1:
                    for j in group:
                        center_ref[j - 1] = center(j - 1)
                        bwd_ref[j - 1] = fwd_ref[j - 1].T
                for j, inverse in zip(group, inverses([center_ref[j] for j in group], len(group) <= 2)):
                    inv_ref[j] = inverse

        @pl.when(always)
        def _(odd=odd, gap=gap, slot=slot):
            for k, j in enumerate(odd):
                low, high = j - gap, j + gap
                sources = jnp.concatenate(
                    [bwd_ref[low], fwd_ref[j], padded(vec_ref[j : j + 1])], axis=0
                )
                z, gram = eliminated(inv_ref[j], sources)
                z_ref[slot + k] = z
                center_ref[low] = center_ref[low] - gram[0:n, 0:n]
                center_ref[high] = center_ref[high] - gram[n : 2 * n, n : 2 * n]
                vec_ref[low : low + 1] = vec_ref[low : low + 1] + gram[2 * n : 2 * n + 1, 0:n]
                vec_ref[high : high + 1] = (
                    vec_ref[high : high + 1] + gram[2 * n : 2 * n + 1, n : 2 * n]
                )
                fwd_ref[low] = gram[n : 2 * n, 0:n]
                bwd_ref[low] = gram[0:n, n : 2 * n]

        level_out = pltpu.make_async_copy(
            z_ref.at[slot : slot + len(odd)],
            z_hbm.at[slot : slot + len(odd)],
            sems.at[3 + len(leaving)],
        )
        level_out.start()
        leaving.append(level_out)
        slot += len(odd)
        gap *= 2
    is_left = bit_of("tm", 0) == 0
    alpha, gamma, u, v = center_ref[0], center_ref[steps], vec_ref[0:1], vec_ref[steps : steps + 1]
    write_near(is_left, near_ref, alpha, gamma, u, v)
    write_far(is_left, far_ref, alpha, gamma, bwd_ref[0], fwd_ref[0], u, v)
    for level_out in leaving:
        level_out.wait()


def inverse_kernel(near_ref, came_near_ref, inv_ref):
    n = near_ref.shape[1]
    inv_ref[...] = inverses([near_ref[0:n] + came_near_ref[0:n]], True)[0]


def parts(level, far_ref, came_far_ref):
    n = far_ref.shape[1]
    is_left = bit_of("tm", level) == 0

    def part(lo, hi):
        m, t = far_ref[lo:hi], came_far_ref[lo:hi]
        return jnp.where(is_left, m, t), jnp.where(is_left, t, m)

    return (*part(0, n), *part(n, 2 * n), *part(2 * n, 2 * n + ROWS))


def near_kernel(level, inv_ref, near_ref, came_near_ref, far_ref, came_far_ref, near_out):
    n = near_ref.shape[1]
    alpha, gamma, beta_low, beta_high, u, v = parts(level, far_ref, came_far_ref)
    next_left = bit_of("tm", level + 1) == 0
    beta = jnp.where(next_left, beta_high, beta_low)
    target = near_ref[n : n + ROWS] + came_near_ref[n : n + ROWS]
    gram = dot(
        dot(jnp.concatenate([beta, target], axis=0), inv_ref[...]), beta, ((1,), (1,))
    )
    near_out[0:n] = jnp.where(next_left, gamma, alpha) - gram[0:n]
    near_out[n : n + ROWS] = jnp.where(next_left, v, u) + gram[n : n + ROWS]


def merged(level, inv_ref, near_ref, came_near_ref, far_ref, came_far_ref):
    n = near_ref.shape[1]
    alpha, gamma, beta_low, beta_high, u, v = parts(level, far_ref, came_far_ref)
    target = near_ref[n : n + ROWS] + came_near_ref[n : n + ROWS]
    z, gram = eliminated(inv_ref[...], jnp.concatenate([beta_low, beta_high, target], axis=0))
    return (
        z,
        alpha - gram[0:n, 0:n],
        gamma - gram[n : 2 * n, n : 2 * n],
        gram[0:n, n : 2 * n],
        gram[n : 2 * n, 0:n],
        u[0:1] + gram[2 * n : 2 * n + 1, 0:n],
        v[0:1] + gram[2 * n : 2 * n + 1, n : 2 * n],
    )


def far_kernel(level, *refs):
    far_out, z_ref = refs[6:]
    z, alpha, gamma, beta_t, beta, u, v = merged(level, *refs[:5])
    z_ref[...] = z
    write_far(bit_of("tm", level + 1) == 0, far_out, alpha, gamma, beta_t, beta, u, v)


def closing_kernel(level, *refs):
    inv_ref, near_ref, came_near_ref, far_ref, came_far_ref, small_ref, z_ref, first_ref = refs
    n = near_ref.shape[1]
    alpha, gamma, beta_low, beta_high, u, v = parts(level, far_ref, came_far_ref)
    target = near_ref[n : n + ROWS] + came_near_ref[n : n + ROWS]
    z_low = dot(jnp.concatenate([beta_low, target], axis=0), inv_ref[...])
    gram = dot(z_low, beta_low, ((1,), (1,)))
    alpha = alpha - gram[0:n]
    u = u + gram[n : n + ROWS]
    (inverse,) = inverses([alpha], True)
    z_high = dot(beta_high, inv_ref[...])
    z_ref[0:n] = z_low[0:n]
    z_ref[n : 2 * n] = z_high
    z_ref[2 * n : 2 * n + ROWS] = z_low[n : n + ROWS]
    gamma = gamma - dot(z_high, beta_high, ((1,), (1,)))
    beta = dot(z_high, beta_low, ((1,), (1,)))
    v = v + dot(z_low[n : n + ROWS], beta_high, ((1,), (1,)))
    first = dot(jnp.concatenate([beta, u], axis=0), inverse)
    first_ref[...] = first
    gram = dot(first, beta, ((1,), (1,)))
    is_lower = bit_of("tm", level + 1) == 0
    small_ref[0:n] = jnp.where(is_lower, gamma - gram[0:n], alpha)
    small_ref[n : n + ROWS] = jnp.where(is_lower, v + gram[n : n + ROWS], u)


def between(z, low, high):
    n = z.shape[1]
    constant = jnp.concatenate([jnp.zeros((2 * n, n), jnp.float32), z[2 * n :]], axis=0)
    return constant + dot(jnp.concatenate([low, high], axis=1), z[0 : 2 * n])


def compose_kernel(levels, steps, *refs):
    z_refs, local_ref, map_ref = refs[: levels - 1], refs[levels - 1], refs[levels]
    n = local_ref.shape[2]
    shape = (2 * n + ROWS, n)
    row_id = lax.broadcasted_iota(jnp.int32, shape, 0)
    lane_id = lax.broadcasted_iota(jnp.int32, shape, 1)
    low = jnp.where(row_id == lane_id, 1.0, 0.0)
    high = jnp.where(row_id == lane_id + n, 1.0, 0.0)
    for level in range(levels - 2, -1, -1):
        z = z_refs[level][...]
        middle = z if level == levels - 2 else between(z, low, high)
        is_left = bit_of("tm", level) == 0
        low, high = jnp.where(is_left, low, middle), jnp.where(is_left, middle, high)
    states = {0: low, steps: high}
    slot = steps - 1
    gap = steps
    while gap > 1:
        slot -= steps // gap
        for k, start in enumerate(range(0, steps, gap)):
            states[start + gap // 2] = between(
                local_ref[slot + k], states[start], states[start + gap]
            )
        gap //= 2
    for t in range(steps):
        map_ref[:, t * n : (t + 1) * n] = states[t]


def final_kernel(levels, steps, mine_ref, theirs_ref, first_ref, map_ref, out_ref):
    n = mine_ref.shape[1]
    (inverse,) = inverses([mine_ref[0:n] + theirs_ref[0:n]], True)
    middle = dot(mine_ref[n : n + 1] + theirs_ref[n : n + 1], inverse)
    first = first_ref[n : n + 1] + dot(middle, first_ref[0:n])
    is_lower = bit_of("tm", levels - 1) == 0
    low = jnp.where(is_lower, first, middle)
    high = jnp.where(is_lower, middle, 0.0)
    states = map_ref[2 * n : 2 * n + 1] + dot(
        jnp.concatenate([low, high], axis=1), map_ref[0 : 2 * n]
    )
    for t in range(steps):
        out_ref[t : t + 1] = states[:, t * n : (t + 1) * n]


def local_call(steps, n, name):
    small = jax.ShapeDtypeStruct((n + ROWS, n), jnp.float32)
    large = jax.ShapeDtypeStruct((2 * n + ROWS, n), jnp.float32)
    return pl.pallas_call(
        local_kernel,
        out_shape=(small, large, jax.ShapeDtypeStruct((steps - 1,) + large.shape, jnp.float32)),
        in_specs=[pl.BlockSpec(memory_space=pltpu.HBM)] * 3,
        out_specs=(
            pl.BlockSpec(memory_space=pltpu.VMEM),
            pl.BlockSpec(memory_space=pltpu.VMEM),
            pl.BlockSpec(memory_space=pltpu.HBM),
        ),
        scratch_shapes=[
            pltpu.VMEM((steps - 1,) + large.shape, jnp.float32),
            pltpu.VMEM((steps, n), jnp.float32),
            pltpu.VMEM((steps, n), jnp.float32),
            pltpu.VMEM((steps + 1, n, n), jnp.float32),
            pltpu.VMEM((steps, n, n), jnp.float32),
            pltpu.VMEM((steps, n, n), jnp.float32),
            pltpu.VMEM((steps, n, n), jnp.float32),
            pltpu.VMEM((2 * steps, n), jnp.float32),
            pltpu.SemaphoreType.DMA((3 + steps.bit_length(),)),
        ],
        compiler_params=pltpu.CompilerParams(vmem_limit_bytes=60 * 2**20),
        name=name,
    )


def body(transition, obs_precision, observations):
    steps, n = obs_precision.shape
    devices = lax.axis_size("tm")
    levels = devices.bit_length() - 1
    params = pltpu.CompilerParams(vmem_limit_bytes=48 * 2**20)
    small = jax.ShapeDtypeStruct((n + ROWS, n), jnp.float32)
    large = jax.ShapeDtypeStruct((2 * n + ROWS, n), jnp.float32)
    square = jax.ShapeDtypeStruct((n, n), jnp.float32)
    near, far, local_z = local_call(steps, n, "local")(transition, obs_precision, observations)
    zs = []

    def exchanged(array, level):
        return lax.ppermute(array, "tm", [(i, i ^ 2**level) for i in range(devices)])

    def called(kernel, out_shape, name, flops, *arrays):
        whole = pl.BlockSpec(memory_space=pltpu.VMEM)
        unread = pl.BlockSpec(memory_space=pl.ANY)
        return pl.pallas_call(
            kernel,
            out_shape=out_shape,
            in_specs=[whole] * 5 + [unread] if len(arrays) == 6 else [whole] * len(arrays),
            compiler_params=params,
            cost_estimate=pl.CostEstimate(
                flops=flops, bytes_accessed=12 * n * n, transcendentals=0
            ),
            name=name,
        )(*arrays)

    for level in range(levels - 1):
        came_near = exchanged(near, level)
        came_far = exchanged(far, level)
        inverse = called(inverse_kernel, square, "inverse", 3000 * n**3, near, came_near)
        held = (inverse, near, came_near, far, came_far)
        if level < levels - 2:
            near = called(
                functools.partial(near_kernel, level), small, "near", 500 * n**3, *held
            )
            far, z = called(
                functools.partial(far_kernel, level), (large, large), "far", 700 * n**3, *held, near
            )
        else:
            near, z, first = called(
                functools.partial(closing_kernel, level), (small, large, small), "closing", 2000 * n**3, *held
            )
        zs.append(z)
    states_map = pl.pallas_call(
        functools.partial(compose_kernel, levels, steps),
        out_shape=jax.ShapeDtypeStruct((2 * n + ROWS, steps * n), jnp.float32),
        compiler_params=params,
        cost_estimate=pl.CostEstimate(
            flops=2000 * n**3, bytes_accessed=32 * steps * n * n, transcendentals=0
        ),
        name="compose",
    )(*zs, local_z)
    return pl.pallas_call(
        functools.partial(final_kernel, levels, steps),
        out_shape=jax.ShapeDtypeStruct((steps, n), jnp.float32),
        compiler_params=params,
        name="final",
    )(near, exchanged(near, levels - 1), first, states_map)


def solution(mesh):
    return jax.shard_map(
        body,
        mesh=mesh,
        in_specs=(P("tm", None, None), P("tm", None), P("tm", None)),
        out_specs=P("tm", None),
        check_vma=False,
    )
```

```python
import functools

import jax
import jax.numpy as jnp
from jax import lax
from jax.experimental import pallas as pl
from jax.experimental.pallas import tpu as pltpu
from jax.sharding import PartitionSpec as P

HIGHEST = lax.Precision.HIGHEST
PANEL = 16
ROWS = 8
SIDE_BY_SIDE = 4


def dot(left, right, contract=((1,), (0,))):
    return lax.dot_general(
        left, right, (contract, ((), ())), precision=HIGHEST, preferred_element_type=jnp.float32
    )


def spread(row):
    return jnp.broadcast_to(row, (ROWS, row.shape[1]))


def lane(tile, column):
    return jnp.broadcast_to(tile[:, column : column + 1], tile.shape)


def summed(terms):
    while len(terms) > 1:
        pairs = [terms[i] + terms[i + 1] for i in range(0, len(terms) - 1, 2)]
        terms = pairs + terms[len(pairs) * 2 :]
    return terms[0]


def panel_solved(cols, rows, masks):
    tiles = len(rows)
    scale = [None] * tiles
    for j in range(len(cols)):
        h, s = divmod(j, ROWS)
        inv = 1.0 / spread(cols[j][h][s : s + 1])
        scale[h] = inv if scale[h] is None else jnp.where(masks[s], inv, scale[h])
        factor = [cols[j][g] * inv for g in range(tiles)]
        factor[h] = jnp.where(masks[s], 0.0, factor[h])
        for c in range(j + 1, len(cols)):
            top = spread(cols[c][h][s : s + 1])
            for g in range(tiles):
                cols[c][g] = cols[c][g] - factor[g] * top
        top = spread(rows[h][s : s + 1])
        for g in range(tiles):
            rows[g] = rows[g] - factor[g] * top
    return [rows[g] * scale[g] for g in range(tiles)]


def inverses(matrices, ahead):
    n = matrices[0].shape[0]
    b = PANEL
    tiles = b // ROWS
    matrices = list(matrices)
    sub_id = lax.broadcasted_iota(jnp.int32, (ROWS, n), 0)
    lane_id = lax.broadcasted_iota(jnp.int32, (ROWS, n), 1)
    full_lane = lax.broadcasted_iota(jnp.int32, (n, n), 1)
    masks = [sub_id == j for j in range(ROWS)]

    def tiled(m, start):
        return [m[start + g * ROWS : start + (g + 1) * ROWS] for g in range(tiles)]

    panels = [tiled(m, 0) for m in matrices]
    for start in range(0, n, b):
        end = start + b
        in_panel = (lane_id >= start) & (lane_id < end)
        in_full = (full_lane >= start) & (full_lane < end)
        ready = []
        for panel in panels:
            cols = [[lane(panel[g], start + c) for g in range(tiles)] for c in range(b)]
            rows = [
                jnp.where(
                    in_panel, jnp.where(lane_id - start == sub_id + ROWS * g, 1.0, 0.0), panel[g]
                )
                for g in range(tiles)
            ]
            ready.append((cols, rows))
        solved = [panel_solved(cols, rows, masks) for cols, rows in ready]
        for q, m in enumerate(matrices):
            if ahead and end < n:
                panels[q] = [
                    jnp.where(in_panel, 0.0, t)
                    - summed(
                        [
                            lane(t, start + j) * spread(solved[q][j // ROWS][j % ROWS : j % ROWS + 1])
                            for j in range(b)
                        ]
                    )
                    for t in tiled(m, end)
                ]
            whole = jnp.concatenate(solved[q], axis=0)
            rest = jnp.where(in_full, 0.0, m) - dot(m[:, start:end], whole)
            parts = [rest[:start]] if start else []
            parts.append(whole)
            if end < n:
                if ahead:
                    parts += panels[q]
                    if end + b < n:
                        parts.append(rest[end + b :])
                else:
                    parts.append(rest[end:])
                    panels[q] = tiled(rest, end)
            matrices[q] = jnp.concatenate(parts, axis=0)
    return matrices


def eliminated(inverse, sources):
    z = dot(sources, inverse)
    return z, dot(z, sources[: sources.shape[0] - ROWS], ((1,), (1,)))


def padded(row):
    return jnp.concatenate([row, jnp.zeros((ROWS - 1, row.shape[1]), jnp.float32)], axis=0)


def write_near(is_left, near_ref, alpha, gamma, u, v):
    n = alpha.shape[0]
    near_ref[0:n] = jnp.where(is_left, gamma, alpha)
    near_ref[n : n + ROWS] = padded(jnp.where(is_left, v, u))


def write_far(is_left, far_ref, alpha, gamma, beta_t, beta, u, v):
    n = alpha.shape[0]
    far_ref[0:n] = jnp.where(is_left, alpha, gamma)
    far_ref[n : 2 * n] = jnp.where(is_left, beta_t, beta)
    far_ref[2 * n : 2 * n + ROWS] = padded(jnp.where(is_left, u, v))


def bit_of(axis, level):
    return lax.rem(lax.div(lax.axis_index(axis), 2**level), 2)


def local_kernel(
    trans_hbm, prec_hbm, obs_hbm, near_ref, far_ref, z_ref,
    prec_ref, obs_ref, center_ref, inv_ref, fwd_ref, bwd_ref, vec_ref, sems,
):
    steps, n = prec_ref.shape
    always = lax.axis_index("tm") >= 0
    copies = [
        pltpu.make_async_copy(trans_hbm, fwd_ref, sems.at[0]),
        pltpu.make_async_copy(prec_hbm, prec_ref, sems.at[1]),
        pltpu.make_async_copy(obs_hbm, obs_ref, sems.at[2]),
    ]
    for copy in copies:
        copy.start()
    for copy in copies:
        copy.wait()

    @pl.when(always)
    def _():
        row_id = lax.broadcasted_iota(jnp.int32, (n, n), 0)
        lane_id = lax.broadcasted_iota(jnp.int32, (n, n), 1)
        for t in range(steps):
            a = fwd_ref[t]
            scale = 1.0 + prec_ref[t : t + 1, :]
            center_ref[t] = jnp.where(row_id == lane_id, scale, 0.0) + dot(a, a, ((0,), (0,)))
            if t % 2 == 0:
                bwd_ref[t] = a.T
        center_ref[steps] = jnp.zeros((n, n), jnp.float32)
        vec_ref[0:steps] = prec_ref[...] * obs_ref[...]
        vec_ref[steps : steps + 1] = jnp.zeros((1, n), jnp.float32)

    slot = 0
    gap = 1
    while gap < steps:
        odd = list(range(gap, steps, 2 * gap))
        for first in range(0, len(odd), SIDE_BY_SIDE):
            group = odd[first : first + SIDE_BY_SIDE]

            @pl.when(always)
            def _(group=group):
                for j, inverse in zip(group, inverses([center_ref[j] for j in group], len(group) <= 2)):
                    inv_ref[j] = inverse

        @pl.when(always)
        def _(odd=odd, gap=gap, slot=slot):
            for k, j in enumerate(odd):
                low, high = j - gap, j + gap
                sources = jnp.concatenate(
                    [bwd_ref[low], fwd_ref[j], padded(vec_ref[j : j + 1])], axis=0
                )
                z, gram = eliminated(inv_ref[j], sources)
                z_ref[slot + k] = z
                center_ref[low] = center_ref[low] - gram[0:n, 0:n]
                center_ref[high] = center_ref[high] - gram[n : 2 * n, n : 2 * n]
                vec_ref[low : low + 1] = vec_ref[low : low + 1] + gram[2 * n : 2 * n + 1, 0:n]
                vec_ref[high : high + 1] = (
                    vec_ref[high : high + 1] + gram[2 * n : 2 * n + 1, n : 2 * n]
                )
                fwd_ref[low] = gram[n : 2 * n, 0:n]
                bwd_ref[low] = gram[0:n, n : 2 * n]

        slot += len(odd)
        gap *= 2
    is_left = bit_of("tm", 0) == 0
    alpha, gamma, u, v = center_ref[0], center_ref[steps], vec_ref[0:1], vec_ref[steps : steps + 1]
    write_near(is_left, near_ref, alpha, gamma, u, v)
    write_far(is_left, far_ref, alpha, gamma, bwd_ref[0], fwd_ref[0], u, v)


def inverse_kernel(near_ref, came_near_ref, inv_ref):
    n = near_ref.shape[1]
    inv_ref[...] = inverses([near_ref[0:n] + came_near_ref[0:n]], True)[0]


def parts(level, far_ref, came_far_ref):
    n = far_ref.shape[1]
    is_left = bit_of("tm", level) == 0

    def part(lo, hi):
        m, t = far_ref[lo:hi], came_far_ref[lo:hi]
        return jnp.where(is_left, m, t), jnp.where(is_left, t, m)

    return (*part(0, n), *part(n, 2 * n), *part(2 * n, 2 * n + ROWS))


def near_kernel(level, inv_ref, near_ref, came_near_ref, far_ref, came_far_ref, near_out):
    n = near_ref.shape[1]
    alpha, gamma, beta_low, beta_high, u, v = parts(level, far_ref, came_far_ref)
    next_left = bit_of("tm", level + 1) == 0
    beta = jnp.where(next_left, beta_high, beta_low)
    target = near_ref[n : n + ROWS] + came_near_ref[n : n + ROWS]
    gram = dot(
        dot(jnp.concatenate([beta, target], axis=0), inv_ref[...]), beta, ((1,), (1,))
    )
    near_out[0:n] = jnp.where(next_left, gamma, alpha) - gram[0:n]
    near_out[n : n + ROWS] = jnp.where(next_left, v, u) + gram[n : n + ROWS]


def merged(level, inv_ref, near_ref, came_near_ref, far_ref, came_far_ref):
    n = near_ref.shape[1]
    alpha, gamma, beta_low, beta_high, u, v = parts(level, far_ref, came_far_ref)
    target = near_ref[n : n + ROWS] + came_near_ref[n : n + ROWS]
    z, gram = eliminated(inv_ref[...], jnp.concatenate([beta_low, beta_high, target], axis=0))
    return (
        z,
        alpha - gram[0:n, 0:n],
        gamma - gram[n : 2 * n, n : 2 * n],
        gram[0:n, n : 2 * n],
        gram[n : 2 * n, 0:n],
        u[0:1] + gram[2 * n : 2 * n + 1, 0:n],
        v[0:1] + gram[2 * n : 2 * n + 1, n : 2 * n],
    )


def far_kernel(level, *refs):
    far_out, z_ref = refs[6:]
    z, alpha, gamma, beta_t, beta, u, v = merged(level, *refs[:5])
    z_ref[...] = z
    write_far(bit_of("tm", level + 1) == 0, far_out, alpha, gamma, beta_t, beta, u, v)


def alpha_kernel(level, inv_ref, near_ref, came_near_ref, far_ref, came_far_ref, near_out):
    n = near_ref.shape[1]
    alpha, _, beta_low, _, u, _ = parts(level, far_ref, came_far_ref)
    target = near_ref[n : n + ROWS] + came_near_ref[n : n + ROWS]
    gram = dot(
        dot(jnp.concatenate([beta_low, target], axis=0), inv_ref[...]), beta_low, ((1,), (1,))
    )
    near_out[0:n] = alpha - gram[0:n]
    near_out[n : n + ROWS] = u + gram[n : n + ROWS]


def closing_kernel(level, *refs):
    inv_ref, near_ref, came_near_ref, far_ref, came_far_ref, alpha_ref = refs[:6]
    small_ref, z_ref, first_ref = refs[6:]
    n = near_ref.shape[1]
    (inverse,) = inverses([alpha_ref[0:n]], True)
    z, _, gamma, _, beta, _, v = merged(level, *refs[:5])
    z_ref[...] = z
    first = dot(jnp.concatenate([beta, alpha_ref[n : n + ROWS]], axis=0), inverse)
    first_ref[...] = first
    gram = dot(first, beta, ((1,), (1,)))
    small_ref[0:n] = gamma - gram[0:n]
    small_ref[n : n + ROWS] = padded(v) + gram[n : n + ROWS]


def middle_kernel(lower_ref, upper_ref, out_ref):
    n = lower_ref.shape[1]
    (inverse,) = inverses([lower_ref[0:n] + upper_ref[0:n]], True)
    out_ref[...] = dot(lower_ref[n : n + ROWS] + upper_ref[n : n + ROWS], inverse)


def between(z, low, high):
    n = z.shape[1]
    constant = jnp.concatenate([jnp.zeros((2 * n, n), jnp.float32), z[2 * n :]], axis=0)
    return constant + dot(jnp.concatenate([low, high], axis=1), z[0 : 2 * n])


def compose_kernel(levels, steps, *refs):
    z_refs, local_ref, map_ref = refs[: levels - 1], refs[levels - 1], refs[levels]
    n = local_ref.shape[2]
    shape = (2 * n + ROWS, n)
    row_id = lax.broadcasted_iota(jnp.int32, shape, 0)
    lane_id = lax.broadcasted_iota(jnp.int32, shape, 1)
    low = jnp.where(row_id == lane_id, 1.0, 0.0)
    high = jnp.where(row_id == lane_id + n, 1.0, 0.0)
    for level in range(levels - 2, -1, -1):
        z = z_refs[level][...]
        middle = z if level == levels - 2 else between(z, low, high)
        is_left = bit_of("tm", level) == 0
        low, high = jnp.where(is_left, low, middle), jnp.where(is_left, middle, high)
    states = {0: low, steps: high}
    slot = steps - 1
    gap = steps
    while gap > 1:
        slot -= steps // gap
        for k, start in enumerate(range(0, steps, gap)):
            states[start + gap // 2] = between(
                local_ref[slot + k], states[start], states[start + gap]
            )
        gap //= 2
    for t in range(steps):
        map_ref[:, t * n : (t + 1) * n] = states[t]


def final_kernel(levels, steps, middle_ref, came_ref, first_ref, map_ref, out_ref):
    n = middle_ref.shape[1]
    is_lower = bit_of("tm", levels - 1) == 0
    middle = jnp.where(is_lower, middle_ref[0:1], came_ref[0:1])
    first = first_ref[n : n + 1] + dot(middle, first_ref[0:n])
    low = jnp.where(is_lower, first, middle)
    high = jnp.where(is_lower, middle, 0.0)
    states = map_ref[2 * n : 2 * n + 1] + dot(
        jnp.concatenate([low, high], axis=1), map_ref[0 : 2 * n]
    )
    for t in range(steps):
        out_ref[t : t + 1] = states[:, t * n : (t + 1) * n]


def local_call(steps, n, name):
    small = jax.ShapeDtypeStruct((n + ROWS, n), jnp.float32)
    large = jax.ShapeDtypeStruct((2 * n + ROWS, n), jnp.float32)
    return pl.pallas_call(
        local_kernel,
        out_shape=(small, large, jax.ShapeDtypeStruct((steps - 1,) + large.shape, jnp.float32)),
        in_specs=[pl.BlockSpec(memory_space=pltpu.HBM)] * 3,
        scratch_shapes=[
            pltpu.VMEM((steps, n), jnp.float32),
            pltpu.VMEM((steps, n), jnp.float32),
            pltpu.VMEM((steps + 1, n, n), jnp.float32),
            pltpu.VMEM((steps, n, n), jnp.float32),
            pltpu.VMEM((steps, n, n), jnp.float32),
            pltpu.VMEM((steps, n, n), jnp.float32),
            pltpu.VMEM((2 * steps, n), jnp.float32),
            pltpu.SemaphoreType.DMA((3,)),
        ],
        compiler_params=pltpu.CompilerParams(vmem_limit_bytes=60 * 2**20),
        name=name,
    )


def body(transition, obs_precision, observations):
    steps, n = obs_precision.shape
    devices = lax.axis_size("tm")
    levels = devices.bit_length() - 1
    params = pltpu.CompilerParams(vmem_limit_bytes=48 * 2**20)
    small = jax.ShapeDtypeStruct((n + ROWS, n), jnp.float32)
    large = jax.ShapeDtypeStruct((2 * n + ROWS, n), jnp.float32)
    square = jax.ShapeDtypeStruct((n, n), jnp.float32)
    near, far, local_z = local_call(steps, n, "local")(transition, obs_precision, observations)
    zs = []
    half = devices // 2

    def exchanged(array, level):
        return lax.ppermute(array, "tm", [(i, i ^ 2**level) for i in range(devices)])

    def called(kernel, out_shape, name, flops, *arrays):
        whole = pl.BlockSpec(memory_space=pltpu.VMEM)
        unread = pl.BlockSpec(memory_space=pl.ANY)
        return pl.pallas_call(
            kernel,
            out_shape=out_shape,
            in_specs=[whole] * 5 + [unread] if name == "far" else [whole] * len(arrays),
            compiler_params=params,
            cost_estimate=pl.CostEstimate(
                flops=flops, bytes_accessed=12 * n * n, transcendentals=0
            ),
            name=name,
        )(*arrays)

    for level in range(levels - 1):
        came_near = exchanged(near, level)
        came_far = exchanged(far, level)
        inverse = called(inverse_kernel, square, "inverse", 3000 * n**3, near, came_near)
        held = (inverse, near, came_near, far, came_far)
        if level < levels - 2:
            near = called(
                functools.partial(near_kernel, level), small, "near", 500 * n**3, *held
            )
            far, z = called(
                functools.partial(far_kernel, level), (large, large), "far", 700 * n**3, *held, near
            )
        else:
            near = called(functools.partial(alpha_kernel, level), small, "near", 500 * n**3, *held)
            upper = lax.ppermute(near, "tm", [(i + half, i) for i in range(half)])
            lower, z, first = called(
                functools.partial(closing_kernel, level),
                (small, large, small),
                "closing",
                3500 * n**3,
                *held,
                near,
            )
        zs.append(z)
    middle = called(
        middle_kernel, jax.ShapeDtypeStruct((ROWS, n), jnp.float32), "middle", 3000 * n**3, lower, upper
    )
    came_middle = lax.ppermute(middle, "tm", [(i, i + half) for i in range(half)])
    states_map = pl.pallas_call(
        functools.partial(compose_kernel, levels, steps),
        out_shape=jax.ShapeDtypeStruct((2 * n + ROWS, steps * n), jnp.float32),
        compiler_params=params,
        cost_estimate=pl.CostEstimate(
            flops=2000 * n**3, bytes_accessed=32 * steps * n * n, transcendentals=0
        ),
        name="compose",
    )(*zs, local_z)
    return pl.pallas_call(
        functools.partial(final_kernel, levels, steps),
        out_shape=jax.ShapeDtypeStruct((steps, n), jnp.float32),
        compiler_params=params,
        name="final",
    )(middle, came_middle, first, states_map)


def solution(mesh):
    return jax.shard_map(
        body,
        mesh=mesh,
        in_specs=(P("tm", None, None), P("tm", None), P("tm", None)),
        out_specs=P("tm", None),
        check_vma=False,
    )
```

```python
import functools

import jax
import jax.numpy as jnp
from jax import lax
from jax.experimental import pallas as pl
from jax.experimental.pallas import tpu as pltpu
from jax.sharding import PartitionSpec as P

HIGHEST = lax.Precision.HIGHEST
PANEL = 16
ROWS = 8
SIDE_BY_SIDE = 4


def dot(left, right, contract=((1,), (0,))):
    return lax.dot_general(
        left, right, (contract, ((), ())), precision=HIGHEST, preferred_element_type=jnp.float32
    )


def spread(row):
    return jnp.broadcast_to(row, (ROWS, row.shape[1]))


def lane(tile, column):
    return jnp.broadcast_to(tile[:, column : column + 1], tile.shape)


def summed(terms):
    while len(terms) > 1:
        pairs = [terms[i] + terms[i + 1] for i in range(0, len(terms) - 1, 2)]
        terms = pairs + terms[len(pairs) * 2 :]
    return terms[0]


def panel_solved(cols, rows, masks):
    tiles = len(rows)
    scale = [None] * tiles
    for j in range(len(cols)):
        h, s = divmod(j, ROWS)
        inv = 1.0 / spread(cols[j][h][s : s + 1])
        scale[h] = inv if scale[h] is None else jnp.where(masks[s], inv, scale[h])
        factor = [cols[j][g] * inv for g in range(tiles)]
        factor[h] = jnp.where(masks[s], 0.0, factor[h])
        for c in range(j + 1, len(cols)):
            top = spread(cols[c][h][s : s + 1])
            for g in range(tiles):
                cols[c][g] = cols[c][g] - factor[g] * top
        top = spread(rows[h][s : s + 1])
        for g in range(tiles):
            rows[g] = rows[g] - factor[g] * top
    return [rows[g] * scale[g] for g in range(tiles)]


def inverses(matrices, ahead):
    n = matrices[0].shape[0]
    b = PANEL
    tiles = b // ROWS
    matrices = list(matrices)
    sub_id = lax.broadcasted_iota(jnp.int32, (ROWS, n), 0)
    lane_id = lax.broadcasted_iota(jnp.int32, (ROWS, n), 1)
    full_lane = lax.broadcasted_iota(jnp.int32, (n, n), 1)
    masks = [sub_id == j for j in range(ROWS)]

    def tiled(m, start):
        return [m[start + g * ROWS : start + (g + 1) * ROWS] for g in range(tiles)]

    panels = [tiled(m, 0) for m in matrices]
    for start in range(0, n, b):
        end = start + b
        in_panel = (lane_id >= start) & (lane_id < end)
        in_full = (full_lane >= start) & (full_lane < end)
        ready = []
        for panel in panels:
            cols = [[lane(panel[g], start + c) for g in range(tiles)] for c in range(b)]
            rows = [
                jnp.where(
                    in_panel, jnp.where(lane_id - start == sub_id + ROWS * g, 1.0, 0.0), panel[g]
                )
                for g in range(tiles)
            ]
            ready.append((cols, rows))
        solved = [panel_solved(cols, rows, masks) for cols, rows in ready]
        for q, m in enumerate(matrices):
            if ahead and end < n:
                panels[q] = [
                    jnp.where(in_panel, 0.0, t)
                    - summed(
                        [
                            lane(t, start + j) * spread(solved[q][j // ROWS][j % ROWS : j % ROWS + 1])
                            for j in range(b)
                        ]
                    )
                    for t in tiled(m, end)
                ]
            whole = jnp.concatenate(solved[q], axis=0)
            rest = jnp.where(in_full, 0.0, m) - dot(m[:, start:end], whole)
            parts = [rest[:start]] if start else []
            parts.append(whole)
            if end < n:
                if ahead:
                    parts += panels[q]
                    if end + b < n:
                        parts.append(rest[end + b :])
                else:
                    parts.append(rest[end:])
                    panels[q] = tiled(rest, end)
            matrices[q] = jnp.concatenate(parts, axis=0)
    return matrices


def eliminated(inverse, sources):
    z = dot(sources, inverse)
    return z, dot(z, sources[: sources.shape[0] - ROWS], ((1,), (1,)))


def padded(row):
    return jnp.concatenate([row, jnp.zeros((ROWS - 1, row.shape[1]), jnp.float32)], axis=0)


def write_near(is_left, near_ref, alpha, gamma, u, v):
    n = alpha.shape[0]
    near_ref[0:n] = jnp.where(is_left, gamma, alpha)
    near_ref[n : n + ROWS] = padded(jnp.where(is_left, v, u))


def write_far(is_left, far_ref, alpha, gamma, beta_t, beta, u, v):
    n = alpha.shape[0]
    far_ref[0:n] = jnp.where(is_left, alpha, gamma)
    far_ref[n : 2 * n] = jnp.where(is_left, beta_t, beta)
    far_ref[2 * n : 2 * n + ROWS] = padded(jnp.where(is_left, u, v))


def bit_of(axis, level):
    return lax.rem(lax.div(lax.axis_index(axis), 2**level), 2)


def local_kernel(
    trans_hbm, prec_hbm, obs_hbm, near_ref, far_ref, z_ref,
    prec_ref, obs_ref, center_ref, inv_ref, fwd_ref, bwd_ref, vec_ref, sems,
):
    steps, n = prec_ref.shape
    always = lax.axis_index("tm") >= 0
    copies = [
        pltpu.make_async_copy(trans_hbm, fwd_ref, sems.at[0]),
        pltpu.make_async_copy(prec_hbm, prec_ref, sems.at[1]),
        pltpu.make_async_copy(obs_hbm, obs_ref, sems.at[2]),
    ]
    for copy in copies:
        copy.start()
    for copy in copies:
        copy.wait()

    @pl.when(always)
    def _():
        row_id = lax.broadcasted_iota(jnp.int32, (n, n), 0)
        lane_id = lax.broadcasted_iota(jnp.int32, (n, n), 1)
        for t in range(steps):
            a = fwd_ref[t]
            scale = 1.0 + prec_ref[t : t + 1, :]
            center_ref[t] = jnp.where(row_id == lane_id, scale, 0.0) + dot(a, a, ((0,), (0,)))
            if t % 2 == 0:
                bwd_ref[t] = a.T
        center_ref[steps] = jnp.zeros((n, n), jnp.float32)
        vec_ref[0:steps] = prec_ref[...] * obs_ref[...]
        vec_ref[steps : steps + 1] = jnp.zeros((1, n), jnp.float32)

    slot = 0
    gap = 1
    while gap < steps:
        odd = list(range(gap, steps, 2 * gap))
        for first in range(0, len(odd), SIDE_BY_SIDE):
            group = odd[first : first + SIDE_BY_SIDE]

            @pl.when(always)
            def _(group=group):
                for j, inverse in zip(group, inverses([center_ref[j] for j in group], len(group) <= 2)):
                    inv_ref[j] = inverse

        @pl.when(always)
        def _(odd=odd, gap=gap, slot=slot):
            for k, j in enumerate(odd):
                low, high = j - gap, j + gap
                sources = jnp.concatenate(
                    [bwd_ref[low], fwd_ref[j], padded(vec_ref[j : j + 1])], axis=0
                )
                z, gram = eliminated(inv_ref[j], sources)
                z_ref[slot + k] = z
                center_ref[low] = center_ref[low] - gram[0:n, 0:n]
                center_ref[high] = center_ref[high] - gram[n : 2 * n, n : 2 * n]
                vec_ref[low : low + 1] = vec_ref[low : low + 1] + gram[2 * n : 2 * n + 1, 0:n]
                vec_ref[high : high + 1] = (
                    vec_ref[high : high + 1] + gram[2 * n : 2 * n + 1, n : 2 * n]
                )
                fwd_ref[low] = gram[n : 2 * n, 0:n]
                bwd_ref[low] = gram[0:n, n : 2 * n]

        slot += len(odd)
        gap *= 2
    is_left = bit_of("tm", 0) == 0
    alpha, gamma, u, v = center_ref[0], center_ref[steps], vec_ref[0:1], vec_ref[steps : steps + 1]
    write_near(is_left, near_ref, alpha, gamma, u, v)
    write_far(is_left, far_ref, alpha, gamma, bwd_ref[0], fwd_ref[0], u, v)


def inverse_kernel(near_ref, came_near_ref, inv_ref):
    n = near_ref.shape[1]
    inv_ref[...] = inverses([near_ref[0:n] + came_near_ref[0:n]], True)[0]


def parts(level, far_ref, came_far_ref):
    n = far_ref.shape[1]
    is_left = bit_of("tm", level) == 0

    def part(lo, hi):
        m, t = far_ref[lo:hi], came_far_ref[lo:hi]
        return jnp.where(is_left, m, t), jnp.where(is_left, t, m)

    return (*part(0, n), *part(n, 2 * n), *part(2 * n, 2 * n + ROWS))


def near_kernel(level, inv_ref, near_ref, came_near_ref, far_ref, came_far_ref, near_out):
    n = near_ref.shape[1]
    alpha, gamma, beta_low, beta_high, u, v = parts(level, far_ref, came_far_ref)
    next_left = bit_of("tm", level + 1) == 0
    beta = jnp.where(next_left, beta_high, beta_low)
    target = near_ref[n : n + ROWS] + came_near_ref[n : n + ROWS]
    gram = dot(
        dot(jnp.concatenate([beta, target], axis=0), inv_ref[...]), beta, ((1,), (1,))
    )
    near_out[0:n] = jnp.where(next_left, gamma, alpha) - gram[0:n]
    near_out[n : n + ROWS] = jnp.where(next_left, v, u) + gram[n : n + ROWS]


def far_kernel(level, *refs):
    inv_ref, near_ref, came_near_ref, far_ref, came_far_ref, _, far_out, z_ref = refs
    n = near_ref.shape[1]
    alpha, gamma, beta_low, beta_high, u, v = parts(level, far_ref, came_far_ref)
    target = near_ref[n : n + ROWS] + came_near_ref[n : n + ROWS]
    z = dot(jnp.concatenate([beta_low, beta_high, target], axis=0), inv_ref[...])
    z_ref[...] = z
    next_left = bit_of("tm", level + 1) == 0
    own = jnp.where(next_left, beta_low, beta_high)
    other = jnp.where(next_left, beta_high, beta_low)
    z_own = jnp.where(next_left, z[0:n], z[n : 2 * n])
    gram = dot(
        jnp.concatenate([z_own, z[2 * n : 2 * n + ROWS]], axis=0),
        jnp.concatenate([own, other], axis=0),
        ((1,), (1,)),
    )
    far_out[0:n] = jnp.where(next_left, alpha, gamma) - gram[0:n, 0:n]
    far_out[n : 2 * n] = gram[0:n, n : 2 * n]
    far_out[2 * n : 2 * n + ROWS] = jnp.where(next_left, u, v) + gram[n : n + ROWS, 0:n]


def closing_kernel(level, *refs):
    inv_ref, near_ref, came_near_ref, far_ref, came_far_ref, small_ref, z_ref, first_ref = refs
    n = near_ref.shape[1]
    alpha, gamma, beta_low, beta_high, u, v = parts(level, far_ref, came_far_ref)
    target = near_ref[n : n + ROWS] + came_near_ref[n : n + ROWS]
    z_low = dot(jnp.concatenate([beta_low, target], axis=0), inv_ref[...])
    gram = dot(z_low, beta_low, ((1,), (1,)))
    alpha = alpha - gram[0:n]
    u = u + gram[n : n + ROWS]
    (inverse,) = inverses([alpha], True)
    z_high = dot(beta_high, inv_ref[...])
    z_ref[0:n] = z_low[0:n]
    z_ref[n : 2 * n] = z_high
    z_ref[2 * n : 2 * n + ROWS] = z_low[n : n + ROWS]
    gamma = gamma - dot(z_high, beta_high, ((1,), (1,)))
    beta = dot(z_high, beta_low, ((1,), (1,)))
    v = v + dot(z_low[n : n + ROWS], beta_high, ((1,), (1,)))
    first = dot(jnp.concatenate([beta, u], axis=0), inverse)
    first_ref[...] = first
    gram = dot(first, beta, ((1,), (1,)))
    is_lower = bit_of("tm", level + 1) == 0
    small_ref[0:n] = jnp.where(is_lower, gamma - gram[0:n], alpha)
    small_ref[n : n + ROWS] = jnp.where(is_lower, v + gram[n : n + ROWS], u)


def between(z, low, high):
    n = low.shape[1]
    return z[2 * n : 2 * n + 1] + dot(jnp.concatenate([low, high], axis=1), z[0 : 2 * n])


def final_kernel(levels, steps, *refs):
    mine_ref, theirs_ref = refs[0:2]
    z_refs = refs[2 : levels + 1]
    first_ref, local_ref, out_ref = refs[levels + 1 :]
    n = mine_ref.shape[1]
    (inverse,) = inverses([mine_ref[0:n] + theirs_ref[0:n]], True)
    middle = dot(mine_ref[n : n + 1] + theirs_ref[n : n + 1], inverse)
    first = first_ref[n : n + 1] + dot(middle, first_ref[0:n])
    is_lower = bit_of("tm", levels - 1) == 0
    low = jnp.where(is_lower, first, middle)
    high = jnp.where(is_lower, middle, 0.0)
    for level in range(levels - 2, -1, -1):
        middle = between(z_refs[level], low, high)
        is_left = bit_of("tm", level) == 0
        low, high = jnp.where(is_left, low, middle), jnp.where(is_left, middle, high)
    states = {0: low, steps: high}
    slot = steps - 1
    gap = steps
    while gap > 1:
        slot -= steps // gap
        for k, start in enumerate(range(0, steps, gap)):
            states[start + gap // 2] = between(
                local_ref.at[slot + k], states[start], states[start + gap]
            )
        gap //= 2
    out_ref[...] = jnp.concatenate([states[t] for t in range(steps)], axis=0)


def local_call(steps, n, name):
    small = jax.ShapeDtypeStruct((n + ROWS, n), jnp.float32)
    large = jax.ShapeDtypeStruct((2 * n + ROWS, n), jnp.float32)
    return pl.pallas_call(
        local_kernel,
        out_shape=(small, large, jax.ShapeDtypeStruct((steps - 1,) + large.shape, jnp.float32)),
        in_specs=[pl.BlockSpec(memory_space=pltpu.HBM)] * 3,
        scratch_shapes=[
            pltpu.VMEM((steps, n), jnp.float32),
            pltpu.VMEM((steps, n), jnp.float32),
            pltpu.VMEM((steps + 1, n, n), jnp.float32),
            pltpu.VMEM((steps, n, n), jnp.float32),
            pltpu.VMEM((steps, n, n), jnp.float32),
            pltpu.VMEM((steps, n, n), jnp.float32),
            pltpu.VMEM((2 * steps, n), jnp.float32),
            pltpu.SemaphoreType.DMA((3,)),
        ],
        compiler_params=pltpu.CompilerParams(vmem_limit_bytes=60 * 2**20),
        name=name,
    )


def body(transition, obs_precision, observations):
    steps, n = obs_precision.shape
    devices = lax.axis_size("tm")
    levels = devices.bit_length() - 1
    params = pltpu.CompilerParams(vmem_limit_bytes=48 * 2**20)
    small = jax.ShapeDtypeStruct((n + ROWS, n), jnp.float32)
    large = jax.ShapeDtypeStruct((2 * n + ROWS, n), jnp.float32)
    square = jax.ShapeDtypeStruct((n, n), jnp.float32)
    near, far, local_z = local_call(steps, n, "local")(transition, obs_precision, observations)
    zs = []

    def exchanged(array, level):
        return lax.ppermute(array, "tm", [(i, i ^ 2**level) for i in range(devices)])

    def called(kernel, out_shape, name, flops, *arrays):
        whole = pl.BlockSpec(memory_space=pltpu.VMEM)
        unread = pl.BlockSpec(memory_space=pl.ANY)
        return pl.pallas_call(
            kernel,
            out_shape=out_shape,
            in_specs=[whole] * 5 + [unread] if len(arrays) == 6 else [whole] * len(arrays),
            compiler_params=params,
            cost_estimate=pl.CostEstimate(
                flops=flops, bytes_accessed=12 * n * n, transcendentals=0
            ),
            name=name,
        )(*arrays)

    for level in range(levels - 1):
        came_near = exchanged(near, level)
        came_far = exchanged(far, level)
        inverse = called(inverse_kernel, square, "inverse", 3000 * n**3, near, came_near)
        held = (inverse, near, came_near, far, came_far)
        if level < levels - 2:
            near = called(
                functools.partial(near_kernel, level), small, "near", 500 * n**3, *held
            )
            far, z = called(
                functools.partial(far_kernel, level), (large, large), "far", 700 * n**3, *held, near
            )
        else:
            near, z, first = called(
                functools.partial(closing_kernel, level), (small, large, small), "closing", 2000 * n**3, *held
            )
        zs.append(z)
    return pl.pallas_call(
        functools.partial(final_kernel, levels, steps),
        out_shape=jax.ShapeDtypeStruct((steps, n), jnp.float32),
        compiler_params=params,
        name="final",
    )(near, exchanged(near, levels - 1), *zs, first, local_z)


def solution(mesh):
    return jax.shard_map(
        body,
        mesh=mesh,
        in_specs=(P("tm", None, None), P("tm", None), P("tm", None)),
        out_specs=P("tm", None),
        check_vma=False,
    )
```

```python
import functools

import jax
import jax.numpy as jnp
from jax import lax
from jax.experimental import pallas as pl
from jax.experimental.pallas import tpu as pltpu
from jax.sharding import PartitionSpec as P

HIGHEST = lax.Precision.HIGHEST
PANEL = 16
ROWS = 8
SIDE_BY_SIDE = 4


def dot(left, right, contract=((1,), (0,))):
    return lax.dot_general(
        left, right, (contract, ((), ())), precision=HIGHEST, preferred_element_type=jnp.float32
    )


def spread(row):
    return jnp.broadcast_to(row, (ROWS, row.shape[1]))


def lane(tile, column):
    return jnp.broadcast_to(tile[:, column : column + 1], tile.shape)


def summed(terms):
    while len(terms) > 1:
        pairs = [terms[i] + terms[i + 1] for i in range(0, len(terms) - 1, 2)]
        terms = pairs + terms[len(pairs) * 2 :]
    return terms[0]


def panel_solved(cols, rows, masks):
    tiles = len(rows)
    scale = [None] * tiles
    for j in range(len(cols)):
        h, s = divmod(j, ROWS)
        inv = 1.0 / spread(cols[j][h][s : s + 1])
        scale[h] = inv if scale[h] is None else jnp.where(masks[s], inv, scale[h])
        factor = [cols[j][g] * inv for g in range(tiles)]
        factor[h] = jnp.where(masks[s], 0.0, factor[h])
        for c in range(j + 1, len(cols)):
            top = spread(cols[c][h][s : s + 1])
            for g in range(tiles):
                cols[c][g] = cols[c][g] - factor[g] * top
        top = spread(rows[h][s : s + 1])
        for g in range(tiles):
            rows[g] = rows[g] - factor[g] * top
    return [rows[g] * scale[g] for g in range(tiles)]


def inverses(matrices, ahead):
    n = matrices[0].shape[0]
    b = PANEL
    tiles = b // ROWS
    matrices = list(matrices)
    sub_id = lax.broadcasted_iota(jnp.int32, (ROWS, n), 0)
    lane_id = lax.broadcasted_iota(jnp.int32, (ROWS, n), 1)
    full_lane = lax.broadcasted_iota(jnp.int32, (n, n), 1)
    masks = [sub_id == j for j in range(ROWS)]

    def tiled(m, start):
        return [m[start + g * ROWS : start + (g + 1) * ROWS] for g in range(tiles)]

    panels = [tiled(m, 0) for m in matrices]
    for start in range(0, n, b):
        end = start + b
        in_panel = (lane_id >= start) & (lane_id < end)
        in_full = (full_lane >= start) & (full_lane < end)
        ready = []
        for panel in panels:
            cols = [[lane(panel[g], start + c) for g in range(tiles)] for c in range(b)]
            rows = [
                jnp.where(
                    in_panel, jnp.where(lane_id - start == sub_id + ROWS * g, 1.0, 0.0), panel[g]
                )
                for g in range(tiles)
            ]
            ready.append((cols, rows))
        solved = [panel_solved(cols, rows, masks) for cols, rows in ready]
        for q, m in enumerate(matrices):
            if ahead and end < n:
                panels[q] = [
                    jnp.where(in_panel, 0.0, t)
                    - summed(
                        [
                            lane(t, start + j) * spread(solved[q][j // ROWS][j % ROWS : j % ROWS + 1])
                            for j in range(b)
                        ]
                    )
                    for t in tiled(m, end)
                ]
            whole = jnp.concatenate(solved[q], axis=0)
            rest = jnp.where(in_full, 0.0, m) - dot(m[:, start:end], whole)
            parts = [rest[:start]] if start else []
            parts.append(whole)
            if end < n:
                if ahead:
                    parts += panels[q]
                    if end + b < n:
                        parts.append(rest[end + b :])
                else:
                    parts.append(rest[end:])
                    panels[q] = tiled(rest, end)
            matrices[q] = jnp.concatenate(parts, axis=0)
    return matrices


def padded(row):
    return jnp.concatenate([row, jnp.zeros((ROWS - 1, row.shape[1]), jnp.float32)], axis=0)


def write_near(is_left, near_ref, alpha, gamma, u, v):
    n = alpha.shape[0]
    near_ref[0:n] = jnp.where(is_left, gamma, alpha)
    near_ref[n : n + ROWS] = padded(jnp.where(is_left, v, u))


def write_far(is_left, far_ref, alpha, gamma, beta_t, beta, u, v):
    n = alpha.shape[0]
    far_ref[0:n] = jnp.where(is_left, alpha, gamma)
    far_ref[n : 2 * n] = jnp.where(is_left, beta_t, beta)
    far_ref[2 * n : 2 * n + ROWS] = padded(jnp.where(is_left, u, v))


def bit_of(axis, level):
    return lax.rem(lax.div(lax.axis_index(axis), 2**level), 2)


def local_kernel(
    trans_hbm, prec_hbm, obs_hbm, near_ref, far_ref, z_ref,
    prec_ref, obs_ref, center_ref, inv_ref, fwd_ref, bwd_ref, vec_ref, sems,
):
    steps, n = prec_ref.shape
    always = lax.axis_index("tm") >= 0
    copies = [
        pltpu.make_async_copy(trans_hbm, fwd_ref, sems.at[0]),
        pltpu.make_async_copy(prec_hbm, prec_ref, sems.at[1]),
        pltpu.make_async_copy(obs_hbm, obs_ref, sems.at[2]),
    ]
    for copy in copies:
        copy.start()
    for copy in copies:
        copy.wait()

    @pl.when(always)
    def _():
        row_id = lax.broadcasted_iota(jnp.int32, (n, n), 0)
        lane_id = lax.broadcasted_iota(jnp.int32, (n, n), 1)
        for t in range(steps):
            a = fwd_ref[t]
            scale = 1.0 + prec_ref[t : t + 1, :]
            center_ref[t] = jnp.where(row_id == lane_id, scale, 0.0) + dot(a, a, ((0,), (0,)))
            if t % 2 == 0:
                bwd_ref[t] = a.T
        center_ref[steps] = jnp.zeros((n, n), jnp.float32)
        vec_ref[0:steps] = prec_ref[...] * obs_ref[...]
        vec_ref[steps : steps + 1] = jnp.zeros((1, n), jnp.float32)

    slot = 0
    gap = 1
    while gap < steps:
        odd = list(range(gap, steps, 2 * gap))
        for first in range(0, len(odd), SIDE_BY_SIDE):
            group = odd[first : first + SIDE_BY_SIDE]

            @pl.when(always)
            def _(group=group):
                for j, inverse in zip(group, inverses([center_ref[j] for j in group], len(group) <= 2)):
                    inv_ref[j] = inverse

        @pl.when(always)
        def _(odd=odd, gap=gap, slot=slot):
            for k, j in enumerate(odd):
                low, high = j - gap, j + gap
                sources = jnp.concatenate(
                    [bwd_ref[low], fwd_ref[j], padded(vec_ref[j : j + 1])], axis=0
                )
                z = dot(sources, inv_ref[j])
                z_ref[slot + k] = z
                pair = sources[0 : 2 * n]
                if len(odd) == 1:
                    gram = dot(z, pair, ((1,), (1,)))
                    low_part, high_part = gram[0:n, 0:n], gram[n : 2 * n, n : 2 * n]
                    vec_part = gram[2 * n : 2 * n + 1]
                    fwd_ref[low] = gram[n : 2 * n, 0:n]
                    bwd_ref[low] = gram[0:n, n : 2 * n]
                else:
                    near_rows = z[0:n] if k % 2 == 0 else z[n : 2 * n]
                    gram = dot(
                        jnp.concatenate([near_rows, z[2 * n :]], axis=0), pair, ((1,), (1,))
                    )
                    vec_part = gram[n : n + 1]
                    if k % 2 == 0:
                        low_part = gram[0:n, 0:n]
                        high_part = dot(z[n : 2 * n], pair[n:], ((1,), (1,)))
                        bwd_ref[low] = gram[0:n, n : 2 * n]
                    else:
                        low_part = dot(z[0:n], pair[0:n], ((1,), (1,)))
                        high_part = gram[0:n, n : 2 * n]
                        fwd_ref[low] = gram[0:n, 0:n]
                center_ref[low] = center_ref[low] - low_part
                center_ref[high] = center_ref[high] - high_part
                vec_ref[low : low + 1] = vec_ref[low : low + 1] + vec_part[:, 0:n]
                vec_ref[high : high + 1] = vec_ref[high : high + 1] + vec_part[:, n : 2 * n]

        slot += len(odd)
        gap *= 2
    is_left = bit_of("tm", 0) == 0
    alpha, gamma, u, v = center_ref[0], center_ref[steps], vec_ref[0:1], vec_ref[steps : steps + 1]
    write_near(is_left, near_ref, alpha, gamma, u, v)
    write_far(is_left, far_ref, alpha, gamma, bwd_ref[0], fwd_ref[0], u, v)


def inverse_kernel(near_ref, came_near_ref, inv_ref):
    n = near_ref.shape[1]
    inv_ref[...] = inverses([near_ref[0:n] + came_near_ref[0:n]], True)[0]


def parts(level, far_ref, came_far_ref):
    n = far_ref.shape[1]
    is_left = bit_of("tm", level) == 0

    def part(lo, hi):
        m, t = far_ref[lo:hi], came_far_ref[lo:hi]
        return jnp.where(is_left, m, t), jnp.where(is_left, t, m)

    return (*part(0, n), *part(n, 2 * n), *part(2 * n, 2 * n + ROWS))


def near_kernel(level, inv_ref, near_ref, came_near_ref, far_ref, came_far_ref, near_out):
    n = near_ref.shape[1]
    alpha, gamma, beta_low, beta_high, u, v = parts(level, far_ref, came_far_ref)
    next_left = bit_of("tm", level + 1) == 0
    beta = jnp.where(next_left, beta_high, beta_low)
    target = near_ref[n : n + ROWS] + came_near_ref[n : n + ROWS]
    gram = dot(
        dot(jnp.concatenate([beta, target], axis=0), inv_ref[...]), beta, ((1,), (1,))
    )
    near_out[0:n] = jnp.where(next_left, gamma, alpha) - gram[0:n]
    near_out[n : n + ROWS] = jnp.where(next_left, v, u) + gram[n : n + ROWS]


def far_kernel(level, *refs):
    inv_ref, near_ref, came_near_ref, far_ref, came_far_ref, _, far_out, z_ref = refs
    n = near_ref.shape[1]
    alpha, gamma, beta_low, beta_high, u, v = parts(level, far_ref, came_far_ref)
    target = near_ref[n : n + ROWS] + came_near_ref[n : n + ROWS]
    z = dot(jnp.concatenate([beta_low, beta_high, target], axis=0), inv_ref[...])
    z_ref[...] = z
    next_left = bit_of("tm", level + 1) == 0
    own = jnp.where(next_left, beta_low, beta_high)
    other = jnp.where(next_left, beta_high, beta_low)
    z_own = jnp.where(next_left, z[0:n], z[n : 2 * n])
    gram = dot(
        jnp.concatenate([z_own, z[2 * n : 2 * n + ROWS]], axis=0),
        jnp.concatenate([own, other], axis=0),
        ((1,), (1,)),
    )
    far_out[0:n] = jnp.where(next_left, alpha, gamma) - gram[0:n, 0:n]
    far_out[n : 2 * n] = gram[0:n, n : 2 * n]
    far_out[2 * n : 2 * n + ROWS] = jnp.where(next_left, u, v) + gram[n : n + ROWS, 0:n]


def closing_kernel(level, *refs):
    inv_ref, near_ref, came_near_ref, far_ref, came_far_ref, small_ref, z_ref, first_ref = refs
    n = near_ref.shape[1]
    alpha, gamma, beta_low, beta_high, u, v = parts(level, far_ref, came_far_ref)
    target = near_ref[n : n + ROWS] + came_near_ref[n : n + ROWS]
    z_low = dot(jnp.concatenate([beta_low, target], axis=0), inv_ref[...])
    gram = dot(z_low, beta_low, ((1,), (1,)))
    alpha = alpha - gram[0:n]
    u = u + gram[n : n + ROWS]
    (inverse,) = inverses([alpha], True)
    z_high = dot(beta_high, inv_ref[...])
    z_ref[0:n] = z_low[0:n]
    z_ref[n : 2 * n] = z_high
    z_ref[2 * n : 2 * n + ROWS] = z_low[n : n + ROWS]
    gamma = gamma - dot(z_high, beta_high, ((1,), (1,)))
    beta = dot(z_high, beta_low, ((1,), (1,)))
    v = v + dot(z_low[n : n + ROWS], beta_high, ((1,), (1,)))
    first = dot(jnp.concatenate([beta, u], axis=0), inverse)
    first_ref[...] = first
    gram = dot(first, beta, ((1,), (1,)))
    is_lower = bit_of("tm", level + 1) == 0
    small_ref[0:n] = jnp.where(is_lower, gamma - gram[0:n], alpha)
    small_ref[n : n + ROWS] = jnp.where(is_lower, v + gram[n : n + ROWS], u)


def between(z, low, high):
    n = low.shape[1]
    return z[2 * n : 2 * n + 1] + dot(jnp.concatenate([low, high], axis=1), z[0 : 2 * n])


def final_kernel(levels, steps, *refs):
    mine_ref, theirs_ref = refs[0:2]
    z_refs = refs[2 : levels + 1]
    first_ref, local_ref, out_ref = refs[levels + 1 :]
    n = mine_ref.shape[1]
    (inverse,) = inverses([mine_ref[0:n] + theirs_ref[0:n]], True)
    middle = dot(mine_ref[n : n + 1] + theirs_ref[n : n + 1], inverse)
    first = first_ref[n : n + 1] + dot(middle, first_ref[0:n])
    is_lower = bit_of("tm", levels - 1) == 0
    low = jnp.where(is_lower, first, middle)
    high = jnp.where(is_lower, middle, 0.0)
    for level in range(levels - 2, -1, -1):
        middle = between(z_refs[level], low, high)
        is_left = bit_of("tm", level) == 0
        low, high = jnp.where(is_left, low, middle), jnp.where(is_left, middle, high)
    states = {0: low, steps: high}
    slot = steps - 1
    gap = steps
    while gap > 1:
        slot -= steps // gap
        for k, start in enumerate(range(0, steps, gap)):
            states[start + gap // 2] = between(
                local_ref.at[slot + k], states[start], states[start + gap]
            )
        gap //= 2
    out_ref[...] = jnp.concatenate([states[t] for t in range(steps)], axis=0)


def local_call(steps, n, name):
    small = jax.ShapeDtypeStruct((n + ROWS, n), jnp.float32)
    large = jax.ShapeDtypeStruct((2 * n + ROWS, n), jnp.float32)
    return pl.pallas_call(
        local_kernel,
        out_shape=(small, large, jax.ShapeDtypeStruct((steps - 1,) + large.shape, jnp.float32)),
        in_specs=[pl.BlockSpec(memory_space=pltpu.HBM)] * 3,
        scratch_shapes=[
            pltpu.VMEM((steps, n), jnp.float32),
            pltpu.VMEM((steps, n), jnp.float32),
            pltpu.VMEM((steps + 1, n, n), jnp.float32),
            pltpu.VMEM((steps, n, n), jnp.float32),
            pltpu.VMEM((steps, n, n), jnp.float32),
            pltpu.VMEM((steps, n, n), jnp.float32),
            pltpu.VMEM((2 * steps, n), jnp.float32),
            pltpu.SemaphoreType.DMA((3,)),
        ],
        compiler_params=pltpu.CompilerParams(vmem_limit_bytes=60 * 2**20),
        name=name,
    )


def body(transition, obs_precision, observations):
    steps, n = obs_precision.shape
    devices = lax.axis_size("tm")
    levels = devices.bit_length() - 1
    params = pltpu.CompilerParams(vmem_limit_bytes=48 * 2**20)
    small = jax.ShapeDtypeStruct((n + ROWS, n), jnp.float32)
    large = jax.ShapeDtypeStruct((2 * n + ROWS, n), jnp.float32)
    square = jax.ShapeDtypeStruct((n, n), jnp.float32)
    near, far, local_z = local_call(steps, n, "local")(transition, obs_precision, observations)
    zs = []

    def exchanged(array, level):
        return lax.ppermute(array, "tm", [(i, i ^ 2**level) for i in range(devices)])

    def called(kernel, out_shape, name, flops, *arrays):
        whole = pl.BlockSpec(memory_space=pltpu.VMEM)
        unread = pl.BlockSpec(memory_space=pl.ANY)
        return pl.pallas_call(
            kernel,
            out_shape=out_shape,
            in_specs=[whole] * 5 + [unread] if len(arrays) == 6 else [whole] * len(arrays),
            compiler_params=params,
            cost_estimate=pl.CostEstimate(
                flops=flops, bytes_accessed=12 * n * n, transcendentals=0
            ),
            name=name,
        )(*arrays)

    for level in range(levels - 1):
        came_near = exchanged(near, level)
        came_far = exchanged(far, level)
        inverse = called(inverse_kernel, square, "inverse", 3000 * n**3, near, came_near)
        held = (inverse, near, came_near, far, came_far)
        if level < levels - 2:
            near = called(
                functools.partial(near_kernel, level), small, "near", 500 * n**3, *held
            )
            far, z = called(
                functools.partial(far_kernel, level), (large, large), "far", 700 * n**3, *held, near
            )
        else:
            near, z, first = called(
                functools.partial(closing_kernel, level), (small, large, small), "closing", 2000 * n**3, *held
            )
        zs.append(z)
    return pl.pallas_call(
        functools.partial(final_kernel, levels, steps),
        out_shape=jax.ShapeDtypeStruct((steps, n), jnp.float32),
        compiler_params=params,
        name="final",
    )(near, exchanged(near, levels - 1), *zs, first, local_z)


def solution(mesh):
    return jax.shard_map(
        body,
        mesh=mesh,
        in_specs=(P("tm", None, None), P("tm", None), P("tm", None)),
        out_specs=P("tm", None),
        check_vma=False,
    )
```
